32 devices in a mesh: row: 4 (over y, core), col: 8 (over z, x).
Axes of the slice: x: 2, y: 2, z: 4, core: 2. Of those that a mesh axis runs over, the one named last changes fastest.
Arguments:
- points: float32 [4, 4, 256, 128], P(None, 'row'), may hold values from -1 to 1
- rhs: float32 [4, 4, 256, 256], P(None, 'row', None, 'col'), may hold values from -6 to 6
Outputs:
- factored: float32 [4, 4, 256, 2, 8, 256], P(None, 'row', None, None, 'col')
- solved: float32 [4, 4, 256, 256], P(None, 'row', None, 'col')
The draws below stay inside these ranges and needn't reach their ends.
All inputs are finite; a program needn't handle non-finite values.
Results may differ from the reference program's by a relative error of at most 0.0003.
Values sent between devices are 32-bit elements; how exact they have to be, the bound alone decides.
A program may use at most 64 MiB of HBM per device.

```python
import jax
import jax.numpy as jnp
from jax import lax

F = 128
B = 256
NRHS = 256
PANELS = 2
NT = 16
N_ROW = 4
N_COL = 8


def block_levels(own_key, extent, pieces, least, largest):
    def one(dim, parts):
        heights = jax.random.uniform(jax.random.fold_in(jax.random.fold_in(own_key, 6), dim), (parts,), jnp.float32, least / len(pieces), largest / len(pieces))
        return jnp.repeat(jnp.exp(heights), extent[dim] // parts).reshape((-1,) + (1,) * (len(extent) - dim - 1))

    factor_of = one(*pieces[0])
    for cut in pieces[1:]:
        factor_of = factor_of * one(*cut)
    return factor_of


def centred(own_key, shape, width, bound, pieces=(), kind=jnp.bfloat16):
    values = width * jax.random.normal(own_key, shape, jnp.float32)
    if pieces:
        values = values * block_levels(own_key, shape, pieces, -0.22, 0.18)
    return jnp.clip(values, -bound, bound).astype(kind)


def setup_inputs(seed: int = 0) -> dict:
    key_list = jax.random.split(jax.random.key(seed), 3)
    return {
        "points": jnp.clip(jax.random.uniform(key_list[0], (NT // N_ROW, N_ROW, B, F), jnp.float32, -1.0, 1.0) * block_levels(key_list[0], (NT // N_ROW, N_ROW, B, F), ((1, 4),), -0.4, 0.0), -1.0, 1.0),
        "rhs": centred(key_list[1], (NT // N_ROW, N_ROW, B, NRHS), 1.0, 6.0, ((1, 4), (3, 8)), jnp.float32),
    }


SCALE = 3.0
NUGGET = 1.0
HIGHEST = lax.Precision.HIGHEST

def reference(points, rhs):
    tile_count = points.shape[0] * points.shape[1]
    tile_size = points.shape[2]
    feature_dim = points.shape[3]
    size = tile_count * tile_size
    design = points.reshape(size, feature_dim)
    right_side = rhs.reshape(size, rhs.shape[-1])
    squares = jnp.sum(design * design, axis=1)
    position = jnp.arange(size, dtype=jnp.int32)

    def build_rows(offset):
        segment = lax.dynamic_slice_in_dim(design, offset, tile_size, 0)
        segment_sq = lax.dynamic_slice_in_dim(squares, offset, tile_size, 0)
        inner_prod = jnp.dot(segment, design.T, precision=HIGHEST)
        distance = segment_sq[:, None] + squares[None, :] - 2.0 * inner_prod
        diagonal_hit = ((offset + jnp.arange(tile_size, dtype=jnp.int32))[:, None] == position[None, :]).astype(jnp.float32)
        return jnp.exp(-SCALE / feature_dim * distance) + NUGGET * diagonal_hit
    kernel = lax.map(build_rows, jnp.arange(tile_count, dtype=jnp.int32) * tile_size).reshape(size, size)
    panels = []
    factors = []
    for which_panel in range(PANELS):
        first_row = which_panel * tile_size
        column = kernel[:, first_row:first_row + tile_size]
        for earlier in panels:
            column = column - jnp.dot(earlier, earlier[first_row:first_row + tile_size].T, precision=HIGHEST)
        factor = jnp.linalg.cholesky(column[first_row:first_row + tile_size])
        panel_tile = jax.scipy.linalg.solve_triangular(factor, column.T, lower=True).T
        beneath = (position >= first_row + tile_size)[:, None]
        panel_tile = jnp.where(beneath, panel_tile, 0.0)
        panel_tile = panel_tile.at[first_row:first_row + tile_size].set(factor)
        panels.append(panel_tile)
        factors.append(factor)
    border = PANELS * tile_size
    joined = jnp.concatenate(panels, axis=1)
    trailing = joined[border:]
    schur = kernel[border:, border:] - jnp.dot(trailing, trailing.T, precision=HIGHEST)
    upper_half = jnp.concatenate([joined[:border], jnp.zeros((border, size - border), jnp.float32)], axis=1)
    lower_half = jnp.concatenate([trailing, schur], axis=1)
    factored = jnp.concatenate([upper_half, lower_half], axis=0).reshape(points.shape[0], points.shape[1], tile_size, tile_count // N_COL, N_COL, tile_size)
    answers = []
    for which_panel in range(PANELS):
        first_row = which_panel * tile_size
        segment = right_side[first_row:first_row + tile_size]
        for earlier, answer in zip(panels, answers):
            segment = segment - jnp.dot(earlier[first_row:first_row + tile_size], answer, precision=HIGHEST)
        answers.append(jax.scipy.linalg.solve_triangular(factors[which_panel], segment, lower=True))
    remainder = right_side[border:] - jnp.dot(trailing, jnp.concatenate(answers, axis=0), precision=HIGHEST)
    solved = jnp.concatenate(answers + [remainder], axis=0).reshape(rhs.shape)
    return (factored, solved)
```

```python
import functools

import jax
import jax.numpy as jnp
from jax import lax
from jax.experimental import pallas as pl
from jax.experimental.pallas import tpu as pltpu
from jax.sharding import PartitionSpec as P

PANELS = 2
SCALE = 3.0
NUGGET = 1.0
HIGHEST = lax.Precision.HIGHEST
MESH = pl.DeviceIdType.MESH
F32 = jnp.float32
BF16 = jnp.bfloat16
NB = 128


def split(x):
    hi = x.astype(BF16)
    return hi, (x - hi.astype(F32)).astype(BF16)


def nt(a, b):
    return lax.dot_general(a, b, (((1,), (1,)), ((), ())), preferred_element_type=F32)


def nt3(a, b):
    return nt(a[0], b[0]) + (nt(a[0], b[1]) + nt(a[1], b[0]))


def squared_exp(a, b, b_sq):
    a_sq = jnp.sum(a * a, axis=1, keepdims=True)
    inner = nt3(split(a), split(b))
    return jnp.exp((-SCALE / a.shape[1]) * (a_sq + b_sq - 2.0 * inner))


def row_squares(b):
    ones = jnp.ones((8, b.shape[1]), F32)
    return lax.dot_general(
        ones, b * b, (((1,), (1,)), ((), ())), precision=HIGHEST, preferred_element_type=F32
    )[:1]


def spread(column):
    return jnp.broadcast_to(column, (column.shape[0], 2 * NB))


def base_inverse(block, base):
    eye = (
        lax.broadcasted_iota(jnp.int32, (NB, NB), 0) == lax.broadcasted_iota(jnp.int32, (NB, NB), 1)
    ).astype(F32)
    wide = jnp.concatenate([block, eye], axis=1)
    v = [wide[8 * q : 8 * q + 8] for q in range(NB // 8)]
    for j in range(0, NB, 4):
        q0, s = divmod(j, 8)
        cols = [[spread(v[q][:, j + n : j + n + 1]) for n in range(4)] for q in range(q0, NB // 8)]
        rows = [v[q0][s + n : s + n + 1] for n in range(4)]
        at = [[cols[0][n][s + m : s + m + 1] for n in range(4)] for m in range(4)]

        def pair(r0, r1, a, b, b1, c, where):
            det = a * c - b * b1
            inv_det = 1.0 / det
            e1 = a * r1 - b1 * r0
            rs = lax.rsqrt(a)
            base[where : where + 1, :] = r0 * rs
            base[where + 1 : where + 2, :] = e1 * (lax.rsqrt(det) * rs)
            return a, b, b1, c, inv_det, (c * r0 - b * r1) * inv_det, e1 * inv_det

        a, b, b1, c, inv_det, s0, s1 = pair(
            rows[0], rows[1], at[0][0], at[0][1], at[1][0], at[1][1], j
        )
        u0 = [(c * at[0][n] - b * at[1][n]) * inv_det for n in (2, 3)]
        u1 = [(a * at[1][n] - b1 * at[0][n]) * inv_det for n in (2, 3)]
        r2, r3 = (rows[m] - at[m][0] * s0 - at[m][1] * s1 for m in (2, 3))
        p = [[at[m][n + 2] - at[m][0] * u0[n] - at[m][1] * u1[n] for n in (0, 1)] for m in (2, 3)]
        s2, s3 = pair(r2, r3, p[0][0], p[0][1], p[1][0], p[1][1], j + 2)[5:]
        for q in range(q0 if s == 0 else q0 + 1, NB // 8):
            k0, k1, k2, k3 = cols[q - q0]
            k2 = k2 - k0 * u0[0] - k1 * u1[0]
            k3 = k3 - k0 * u0[1] - k1 * u1[1]
            v[q] = v[q] - k0 * s0 - k1 * s1 - k2 * s2 - k3 * s3
    return base[:, NB:]


def inverse_factor(w, h, base):
    size = h.shape[0]
    for j0 in range(0, size, NB):
        j1 = j0 + NB
        inv = base_inverse(w[j0:j1, j0:j1], base)
        rows = jnp.dot(inv, w[j0:j1, :], precision=HIGHEST, preferred_element_type=F32)
        h[j0:j1, :] = rows[:, size:]
        if j1 < size:
            panel = lax.dot_general(
                w[j1:, j0:j1], inv, (((1,), (1,)), ((), ())), precision=HIGHEST, preferred_element_type=F32
            )
            w[j1:, :] = w[j1:, :] - jnp.dot(
                panel, rows, precision=HIGHEST, preferred_element_type=F32
            )


def factor_kernel(
    rows_n, cols_n, tile_cols, pts, prhs, opiv, ocolp, oh, oy,
    piv, colp, rpiv, base, w, h0, h1, hs, ys, send, recv, local, wsem,
):
    row_id = lax.axis_index("row")
    col_id = lax.axis_index("col")
    stride = cols_n // rows_n

    barrier = pltpu.get_barrier_semaphore()
    for step in range(1, rows_n):
        other = lax.rem(row_id + step, rows_n)
        pl.semaphore_signal(barrier, inc=1, device_id={"row": other}, device_id_type=MESH)

    jobs = [(k % rows_n, pts.at[k // rows_n], piv.at[k]) for k in range(PANELS)]
    jobs += [(k % rows_n, prhs.at[k // rows_n], rpiv.at[k]) for k in range(PANELS)]
    for c2 in range(tile_cols):
        slot = c2 * stride + col_id // rows_n
        jobs.append((lax.rem(col_id, rows_n), pts.at[slot], colp.at[c2]))

    chips = rows_n // 2
    chip, core = row_id // 2, lax.rem(row_id, 2)
    sibling = row_id + 1 - 2 * core

    def half_of(ref, half):
        height = ref.shape[0] // 2
        return ref.at[pl.ds(pl.multiple_of(half * height, height), height)]

    def remote(number, half, dest, slot, relay=False):
        _, src, dst = jobs[number]
        return pltpu.make_async_remote_copy(
            src_ref=half_of(dst if relay else src, half),
            dst_ref=half_of(dst, half),
            send_sem=send.at[number, slot],
            recv_sem=recv.at[number, half],
            device_id={"row": dest},
            device_id_type=MESH,
        )

    def sends(number):
        out = []
        for step in range(1, chips):
            for half in range(2):
                dest = 2 * lax.rem(chip + step, chips) + half
                out.append(remote(number, half, dest, 2 * step + half))
        return out + [remote(number, half, sibling, half) for half in range(2)]

    def own(number):
        _, src, dst = jobs[number]
        return pltpu.make_async_copy(src, dst, local.at[number])

    def when(condition):
        return pl.when(condition)

    def launch(number):
        @when(row_id == jobs[number][0])
        def _():
            for copy in sends(number):
                copy.start()

    def relay(number):
        @when(chip != jobs[number][0] // 2)
        def _():
            copy = remote(number, core, sibling, 0, relay=True)
            copy.wait_recv()
            copy.start()

    def arrive(number):
        owner = jobs[number][0]

        @when(row_id == owner)
        def _():
            own(number).wait()

        @when(sibling == owner)
        def _():
            for half in range(2):
                remote(number, half, sibling, half).wait_recv()

        @when(chip != owner // 2)
        def _():
            remote(number, 1 - core, sibling, 0, relay=True).wait_recv()

    def drain(number):
        owner = jobs[number][0]

        @when(row_id == owner)
        def _():
            for copy in sends(number):
                copy.wait_send()

        @when(chip != owner // 2)
        def _():
            remote(number, core, sibling, 0, relay=True).wait_send()

    for number in range(len(jobs)):
        @when(row_id == jobs[number][0])
        def _(number=number):
            own(number).start()

    pl.semaphore_wait(barrier, rows_n - 1)
    for number in range(len(jobs)):
        launch(number)
    relay(0)
    arrive(0)

    size = piv.shape[1]
    eye = (
        lax.broadcasted_iota(jnp.int32, (size, size), 0) == lax.broadcasted_iota(jnp.int32, (size, size), 1)
    ).astype(F32)
    x0 = piv[0]
    sq0 = row_squares(x0)
    w[:, :size] = squared_exp(x0, x0, sq0) + NUGGET * eye
    w[:, size:] = eye
    inverse_factor(w, h0, base)

    for number in range(1, len(jobs)):
        relay(number)
    for number in range(1, len(jobs)):
        arrive(number)
    writes = [pltpu.make_async_copy(piv, opiv, wsem.at[0]), pltpu.make_async_copy(colp, ocolp, wsem.at[1])]
    for copy in writes:
        copy.start()

    x1 = piv[1]
    sq1 = row_squares(x1)
    h0s = split(h0[...])
    hs[0, 0], hs[0, 1] = h0s
    l10s = split(nt3(split(squared_exp(x1, x0, sq0)), h0s))
    w[:, :size] = squared_exp(x1, x1, sq1) + NUGGET * eye - nt3(l10s, l10s)
    w[:, size:] = eye
    inverse_factor(w, h1, base)
    h1s = split(h1[...])
    hs[1, 0], hs[1, 1] = h1s
    hx = -nn3(split(nn3(h1s, l10s)), h0s)
    hxs = split(hx)
    hs[2, 0], hs[2, 1] = hxs
    writes.append(pltpu.make_async_copy(hs, oh, wsem.at[2]))
    writes[-1].start()
    r0, r1 = split(rpiv[0]), split(rpiv[1])
    ys[:, :size] = nt3(r0, h0s)
    ys[:, size:] = nt3(r0, hxs) + nt3(r1, h1s)
    writes.append(pltpu.make_async_copy(ys, oy, wsem.at[3]))
    writes[-1].start()
    for number in range(len(jobs)):
        drain(number)
    for copy in writes:
        copy.wait()


def nn(a, b):
    return lax.dot_general(a, b, (((1,), (0,)), ((), ())), preferred_element_type=F32)


def nn3(a, b):
    return nn(a[0], b[0]) + (nn(a[0], b[1]) + nn(a[1], b[0]))


def tiles_kernel(
    rows_n, cols_n, hpts, hpiv, hcolp, hrhs, hh, hy, out, solved,
    pts, piv, colp, rhs, hs, ys, lh, ll, stage, rest, sems, osems,
):
    row_id = lax.axis_index("row")
    col_id = lax.axis_index("col")
    copies = [
        pltpu.make_async_copy(src, dst, sems.at[n])
        for n, (src, dst) in enumerate(
            ((hpiv, piv), (hcolp, colp), (hh, hs), (hpts, pts), (hrhs, rhs), (hy, ys))
        )
    ]
    for copy in copies:
        copy.start()
    tile_rows, size, _ = pts.shape
    tile_cols = colp.shape[0]
    row_in = lax.broadcasted_iota(jnp.int32, (size, size), 0)
    col_in = lax.broadcasted_iota(jnp.int32, (size, size), 1)
    eye = (row_in == col_in).astype(F32)
    lower = row_in >= col_in
    for copy in copies:
        copy.wait()
    x0, x1 = piv[0], piv[1]
    sq0, sq1 = row_squares(x0), row_squares(x1)
    h0s, h1s, hxs = ((hs[n, 0], hs[n, 1]) for n in range(3))

    def panels_of(x, tile):
        k0 = split(squared_exp(x, x0, sq0) + jnp.where(tile == 0, NUGGET, 0.0) * eye)
        l0 = nt3(k0, h0s)
        l0 = jnp.where((tile != 0) | lower, l0, 0.0)
        k1 = split(squared_exp(x, x1, sq1) + jnp.where(tile == 1, NUGGET, 0.0) * eye)
        l1 = nt3(k0, hxs) + nt3(k1, h1s)
        l1 = jnp.where((tile > 1) | (lower & (tile == 1)), l1, 0.0)
        return l0, l1

    for c2 in range(tile_cols):
        l0, l1 = panels_of(colp[c2], c2 * cols_n + col_id)
        lh[c2, :, :size], ll[c2, :, :size] = split(l0)
        lh[c2, :, size:], ll[c2, :, size:] = split(l1)
    yv = ys[...]
    y = split(yv)

    writes = []
    for a in range(tile_rows):
        tile = a * rows_n + row_id
        x = pts[a]
        l0, l1 = panels_of(x, tile)
        ls = split(jnp.concatenate([l0, l1], axis=1))
        left = rhs[a] - nt3(y, ls)
        rest[a] = jnp.where(tile == 0, yv[:, :size], jnp.where(tile == 1, yv[:, size:], left))
        for c2 in range(tile_cols):
            tile_c = c2 * cols_n + col_id
            xc = colp[c2]
            k = squared_exp(x, xc, row_squares(xc)) + jnp.where(tile == tile_c, NUGGET, 0.0) * eye
            s = k - nt3(ls, (lh[c2], ll[c2]))
            s = jnp.where(tile >= PANELS, s, 0.0)
            if c2 == 0:
                s = jnp.where(tile_c == 0, l0, jnp.where(tile_c == 1, l1, s))
            for half in range(size // 128):
                stage[a, pl.ds(c2 * (size // 128) + half, size, stride=tile_cols * size // 128), :] = s[
                    :, half * 128 : half * 128 + 128
                ]
        writes.append(pltpu.make_async_copy(stage.at[a], out.at[a], osems.at[a]))
        writes[-1].start()
    writes.append(pltpu.make_async_copy(rest, solved, osems.at[tile_rows]))
    writes[-1].start()
    for copy in writes:
        copy.wait()


def per_device(points, rhs):
    rows_n = lax.axis_size("row")
    cols_n = lax.axis_size("col")
    tile_rows, _, size, feat = points.shape
    width = rhs.shape[-1]
    tile_cols = tile_rows * rows_n // cols_n
    pts = points[:, 0]
    right = rhs[:, 0].swapaxes(1, 2)
    jobs = 2 * PANELS + tile_cols
    hbm = pl.BlockSpec(memory_space=pltpu.HBM)
    piv_s, colp_s = (PANELS, size, feat), (tile_cols, size, feat)
    h_s, y_s = (3, 2, size, size), (width, PANELS * size)
    piv, colp, hs, ys = pl.pallas_call(
        functools.partial(factor_kernel, rows_n, cols_n, tile_cols),
        out_shape=(
            jax.ShapeDtypeStruct(piv_s, F32),
            jax.ShapeDtypeStruct(colp_s, F32),
            jax.ShapeDtypeStruct(h_s, BF16),
            jax.ShapeDtypeStruct(y_s, F32),
        ),
        in_specs=[hbm] * 2,
        out_specs=(hbm,) * 4,
        scratch_shapes=[
            pltpu.VMEM(piv_s, F32),
            pltpu.VMEM(colp_s, F32),
            pltpu.VMEM((PANELS, width, size), F32),
            pltpu.VMEM((NB, 2 * NB), F32),
            pltpu.VMEM((size, 2 * size), F32),
            pltpu.VMEM((size, size), F32),
            pltpu.VMEM((size, size), F32),
            pltpu.VMEM(h_s, BF16),
            pltpu.VMEM(y_s, F32),
            pltpu.SemaphoreType.DMA((jobs, rows_n)),
            pltpu.SemaphoreType.DMA((jobs, 2)),
            pltpu.SemaphoreType.DMA((jobs,)),
            pltpu.SemaphoreType.DMA((4,)),
        ],
        compiler_params=pltpu.CompilerParams(
            collective_id=0, has_side_effects=True, vmem_limit_bytes=62 * 1024 * 1024
        ),
        name="factor",
    )(pts, right)
    out_s = (tile_rows, size * tile_cols * size // 128, 128)
    factored, solved = pl.pallas_call(
        functools.partial(tiles_kernel, rows_n, cols_n),
        out_shape=(
            jax.ShapeDtypeStruct(out_s, F32),
            jax.ShapeDtypeStruct((tile_rows, width, size), F32),
        ),
        in_specs=[hbm] * 6,
        out_specs=(hbm,) * 2,
        scratch_shapes=[
            pltpu.VMEM(pts.shape, F32),
            pltpu.VMEM(piv_s, F32),
            pltpu.VMEM(colp_s, F32),
            pltpu.VMEM(right.shape, F32),
            pltpu.VMEM(h_s, BF16),
            pltpu.VMEM(y_s, F32),
            pltpu.VMEM((tile_cols, size, PANELS * size), BF16),
            pltpu.VMEM((tile_cols, size, PANELS * size), BF16),
            pltpu.VMEM(out_s, F32),
            pltpu.VMEM((tile_rows, width, size), F32),
            pltpu.SemaphoreType.DMA((6,)),
            pltpu.SemaphoreType.DMA((tile_rows + 1,)),
        ],
        compiler_params=pltpu.CompilerParams(vmem_limit_bytes=62 * 1024 * 1024),
        name="tiles",
    )(pts, piv, colp, right, hs, ys)
    factored = factored.reshape(tile_rows, 1, size, tile_cols, 1, size)
    return factored, solved.swapaxes(1, 2)[:, None]


def solution(mesh):
    return jax.shard_map(
        per_device,
        mesh=mesh,
        in_specs=(P(None, "row", None, None), P(None, "row", None, "col")),
        out_specs=(P(None, "row", None, None, "col", None), P(None, "row", None, "col")),
        check_vma=False,
    )
```

```python
import functools

import jax
import jax.numpy as jnp
from jax import lax
from jax.experimental import pallas as pl
from jax.experimental.pallas import tpu as pltpu
from jax.sharding import PartitionSpec as P

PANELS = 2
SCALE = 3.0
NUGGET = 1.0
HIGHEST = lax.Precision.HIGHEST
MESH = pl.DeviceIdType.MESH
F32 = jnp.float32
BF16 = jnp.bfloat16
NB = 128


def split(x):
    hi = x.astype(BF16)
    return hi, (x - hi.astype(F32)).astype(BF16)


def nt(a, b):
    return lax.dot_general(a, b, (((1,), (1,)), ((), ())), preferred_element_type=F32)


def nt3(a, b):
    return nt(a[0], b[0]) + (nt(a[0], b[1]) + nt(a[1], b[0]))


def squared_exp(a, b, b_sq):
    a_sq = jnp.sum(a * a, axis=1, keepdims=True)
    inner = nt3(split(a), split(b))
    return jnp.exp((-SCALE / a.shape[1]) * (a_sq + b_sq - 2.0 * inner))


def row_squares(b):
    ones = jnp.ones((8, b.shape[1]), F32)
    return lax.dot_general(
        ones, b * b, (((1,), (1,)), ((), ())), precision=HIGHEST, preferred_element_type=F32
    )[:1]


def splat(tile, j):
    return jnp.broadcast_to(tile[:, j:j+1], tile.shape)
def rowof(tile, s):
    return jnp.broadcast_to(tile[s:s+1], tile.shape)

def base_inverse(block, width=16, ahead=2):
    lane = lax.broadcasted_iota(jnp.int32, (8, NB), 1)
    sub = lax.broadcasted_iota(jnp.int32, (8, NB), 0)
    v = [block[8 * q : 8 * q + 8] for q in range(NB // 8)]
    rows_n = len(v)
    per = width // 8
    out = []
    for j in range(0, NB, width):
        q0 = j // 8
        near = list(range(q0 + per, min(q0 + per + ahead, rows_n)))
        far = list(range(q0 + per + ahead, rows_n))
        d = [[splat(v[q0+t], j+n) for n in range(width)] for t in range(per)]
        d[0] = [jnp.where(lane >= 0, x, 0.0) for x in d[0]]
        low = [[splat(v[q], j+n) for n in range(width)] for q in near]
        inside = (lane >= j) & (lane < j+width)
        r = [jnp.where(inside, (lane - j == sub + 8*t).astype(F32), v[q0+t]) for t in range(per)]
        f = [None]*per
        S = [None]*width
        us = {}
        for n in range(0, width, 2):
            t, s = divmod(n, 8)
            a, b, c = rowof(d[t][n], s), rowof(d[t][n+1], s), rowof(d[t][n+1], s+1)
            det = a*c - b*b
            inv = 1.0/det
            ai, bi, ci = a*inv, b*inv, c*inv
            r0, r1 = rowof(r[t], s), rowof(r[t], s+1)
            rs = lax.rsqrt(a)
            f0 = r0*rs
            f1 = (a*r1 - b*r0)*(lax.rsqrt(det)*rs)
            f[t] = f0 if f[t] is None else jnp.where(sub == s, f0, f[t])
            f[t] = jnp.where(sub == s+1, f1, f[t])
            S[n], S[n+1] = ci*r0 - bi*r1, ai*r1 - bi*r0
            for m in range(n+2, width):
                x, y = rowof(d[t][m], s), rowof(d[t][m], s+1)
                u0, u1 = ci*x - bi*y, ai*y - bi*x
                us[n, m] = u0, u1
                for tt in range((n+2)//8, per):
                    d[tt][m] = d[tt][m] - (d[tt][n]*u0 + d[tt][n+1]*u1)
            for tt in range((n+2)//8, per):
                r[tt] = r[tt] - (d[tt][n]*S[n] + d[tt][n+1]*S[n+1])
        if near:
            for n in range(width-4, -1, -2):
                for m in range(width-1, n+1, -1):
                    u0, u1 = us[n, m]
                    S[n] = S[n] - u0*S[m]
                    S[n+1] = S[n+1] - u1*S[m]
        for t in range(per):
            out.append(jnp.where(lane <= j + 8*t + sub, f[t], 0.0))
        for i, q in enumerate(near):
            acc = [low[i][n]*S[n] for n in range(4)]
            for n in range(4, width):
                acc[n % 4] = acc[n % 4] + low[i][n]*S[n]
            v[q] = jnp.where(inside, 0.0, v[q]) - ((acc[0]+acc[1])+(acc[2]+acc[3]))
        if far:
            fc = jnp.concatenate(f, axis=0)
            hi = fc.astype(BF16)
            lo = (fc - hi.astype(F32)).astype(BF16)
            up = lax.dot_general(jnp.concatenate([hi, hi, lo], axis=0), jnp.concatenate([hi, lo, hi], axis=0),
                                 (((0,), (0,)), ((), ())), preferred_element_type=F32)
            for q in far:
                v[q] = jnp.where(inside, 0.0, v[q]) - up[8*q:8*q+8]
    return jnp.concatenate(out, axis=0)


def inverse_factor(w, h):
    inv = base_inverse(w[:NB, :NB])
    h[:NB, :NB] = inv
    h[:NB, NB:] = jnp.zeros((NB, w.shape[1] - NB), F32)
    first = split(inv)
    below = split(nt3(split(w[NB:, :NB]), first))
    w[NB:, NB:] = w[NB:, NB:] - nt3(below, below)
    mixed = split(nn3(below, first))
    inv = base_inverse(w[NB:, NB:])
    h[NB:, NB:] = inv
    h[NB:, :NB] = -nn3(split(inv), mixed)


def factor_kernel(
    rows_n, cols_n, tile_cols, pts, prhs, opiv, ocolp, oh, oy,
    piv, colp, rpiv, w, h0, h1, hs, ys, send, recv, local, wsem,
):
    row_id = lax.axis_index("row")
    col_id = lax.axis_index("col")
    stride = cols_n // rows_n

    barrier = pltpu.get_barrier_semaphore()
    for step in range(1, rows_n):
        other = lax.rem(row_id + step, rows_n)
        pl.semaphore_signal(barrier, inc=1, device_id={"row": other}, device_id_type=MESH)

    jobs = [(k % rows_n, pts.at[k // rows_n], piv.at[k]) for k in range(PANELS)]
    jobs += [(k % rows_n, prhs.at[k // rows_n], rpiv.at[k]) for k in range(PANELS)]
    for c2 in range(tile_cols):
        slot = c2 * stride + col_id // rows_n
        jobs.append((lax.rem(col_id, rows_n), pts.at[slot], colp.at[c2]))

    chips = rows_n // 2
    chip, core = row_id // 2, lax.rem(row_id, 2)
    sibling = row_id + 1 - 2 * core

    def half_of(ref, half):
        height = ref.shape[0] // 2
        return ref.at[pl.ds(pl.multiple_of(half * height, height), height)]

    def remote(number, half, dest, slot, relay=False):
        _, src, dst = jobs[number]
        return pltpu.make_async_remote_copy(
            src_ref=half_of(dst if relay else src, half),
            dst_ref=half_of(dst, half),
            send_sem=send.at[number, slot],
            recv_sem=recv.at[number, half],
            device_id={"row": dest},
            device_id_type=MESH,
        )

    def sends(number):
        out = []
        for step in range(1, chips):
            for half in range(2):
                dest = 2 * lax.rem(chip + step, chips) + half
                out.append(remote(number, half, dest, 2 * step + half))
        return out + [remote(number, half, sibling, half) for half in range(2)]

    def own(number):
        _, src, dst = jobs[number]
        return pltpu.make_async_copy(src, dst, local.at[number])

    def when(condition):
        return pl.when(condition)

    def launch(number):
        @when(row_id == jobs[number][0])
        def _():
            for copy in sends(number):
                copy.start()

    def relay(number):
        @when(chip != jobs[number][0] // 2)
        def _():
            copy = remote(number, core, sibling, 0, relay=True)
            copy.wait_recv()
            copy.start()

    def arrive(number):
        owner = jobs[number][0]

        @when(row_id == owner)
        def _():
            own(number).wait()

        @when(sibling == owner)
        def _():
            for half in range(2):
                remote(number, half, sibling, half).wait_recv()

        @when(chip != owner // 2)
        def _():
            remote(number, 1 - core, sibling, 0, relay=True).wait_recv()

    def drain(number):
        owner = jobs[number][0]

        if number:
            @when(row_id == owner)
            def _():
                for copy in sends(number):
                    copy.wait_send()

        @when(chip != owner // 2)
        def _():
            remote(number, core, sibling, 0, relay=True).wait_send()

    for number in range(len(jobs)):
        @when(row_id == jobs[number][0])
        def _(number=number):
            own(number).start()

    pl.semaphore_wait(barrier, rows_n - 1)
    launch(0)
    relay(0)
    arrive(0)

    @when(row_id == jobs[0][0])
    def _():
        for copy in sends(0):
            copy.wait_send()

    for number in range(1, len(jobs)):
        launch(number)

    size = piv.shape[1]
    eye = (
        lax.broadcasted_iota(jnp.int32, (size, size), 0) == lax.broadcasted_iota(jnp.int32, (size, size), 1)
    ).astype(F32)
    x0 = piv[0]
    sq0 = row_squares(x0)
    w[...] = squared_exp(x0, x0, sq0) + NUGGET * eye
    inverse_factor(w, h0)
    h0s = split(h0[...])
    hs[0, 0], hs[0, 1] = h0s

    for number in range(1, len(jobs)):
        relay(number)
    arrive(1)
    x1 = piv[1]
    sq1 = row_squares(x1)
    l10s = split(nt3(split(squared_exp(x1, x0, sq0)), h0s))
    w[...] = squared_exp(x1, x1, sq1) + NUGGET * eye - nt3(l10s, l10s)
    mixed = split(nn3(l10s, h0s))
    inverse_factor(w, h1)

    for number in range(2, len(jobs)):
        arrive(number)
    writes = [pltpu.make_async_copy(piv, opiv, wsem.at[0]), pltpu.make_async_copy(colp, ocolp, wsem.at[1])]
    for copy in writes:
        copy.start()
    h1s = split(h1[...])
    hs[1, 0], hs[1, 1] = h1s
    hxs = split(-nn3(h1s, mixed))
    hs[2, 0], hs[2, 1] = hxs
    writes.append(pltpu.make_async_copy(hs, oh, wsem.at[2]))
    writes[-1].start()
    r0, r1 = split(rpiv[0]), split(rpiv[1])
    ys[:, :size] = nt3(r0, h0s)
    ys[:, size:] = nt3(r0, hxs) + nt3(r1, h1s)
    writes.append(pltpu.make_async_copy(ys, oy, wsem.at[3]))
    writes[-1].start()
    for number in range(len(jobs)):
        drain(number)
    for copy in writes:
        copy.wait()


def nn(a, b):
    return lax.dot_general(a, b, (((1,), (0,)), ((), ())), preferred_element_type=F32)


def nn3(a, b):
    return nn(a[0], b[0]) + (nn(a[0], b[1]) + nn(a[1], b[0]))


def tiles_kernel(
    rows_n, cols_n, hpts, hpiv, hcolp, hrhs, hh, hy, out, solved,
    pts, piv, colp, rhs, hs, ys, lh, ll, stage, rest, sems, osems,
):
    row_id = lax.axis_index("row")
    col_id = lax.axis_index("col")
    copies = [
        pltpu.make_async_copy(src, dst, sems.at[n])
        for n, (src, dst) in enumerate(
            ((hpiv, piv), (hcolp, colp), (hh, hs), (hpts, pts), (hrhs, rhs), (hy, ys))
        )
    ]
    for copy in copies:
        copy.start()
    tile_rows, size, _ = pts.shape
    tile_cols = colp.shape[0]
    row_in = lax.broadcasted_iota(jnp.int32, (size, size), 0)
    col_in = lax.broadcasted_iota(jnp.int32, (size, size), 1)
    eye = (row_in == col_in).astype(F32)
    lower = row_in >= col_in
    for copy in copies:
        copy.wait()
    x0, x1 = piv[0], piv[1]
    sq0, sq1 = row_squares(x0), row_squares(x1)
    h0s, h1s, hxs = ((hs[n, 0], hs[n, 1]) for n in range(3))

    def panels_of(x, tile):
        k0 = split(squared_exp(x, x0, sq0) + jnp.where(tile == 0, NUGGET, 0.0) * eye)
        l0 = nt3(k0, h0s)
        l0 = jnp.where((tile != 0) | lower, l0, 0.0)
        k1 = split(squared_exp(x, x1, sq1) + jnp.where(tile == 1, NUGGET, 0.0) * eye)
        l1 = nt3(k0, hxs) + nt3(k1, h1s)
        l1 = jnp.where((tile > 1) | (lower & (tile == 1)), l1, 0.0)
        return l0, l1

    for c2 in range(tile_cols):
        l0, l1 = panels_of(colp[c2], c2 * cols_n + col_id)
        lh[c2, :, :size], ll[c2, :, :size] = split(l0)
        lh[c2, :, size:], ll[c2, :, size:] = split(l1)
    yv = ys[...]
    y = split(yv)

    writes = []
    for a in range(tile_rows):
        tile = a * rows_n + row_id
        x = pts[a]
        l0, l1 = panels_of(x, tile)
        ls = split(jnp.concatenate([l0, l1], axis=1))
        left = rhs[a] - nt3(y, ls)
        rest[a] = jnp.where(tile == 0, yv[:, :size], jnp.where(tile == 1, yv[:, size:], left))
        for c2 in range(tile_cols):
            tile_c = c2 * cols_n + col_id
            xc = colp[c2]
            k = squared_exp(x, xc, row_squares(xc)) + jnp.where(tile == tile_c, NUGGET, 0.0) * eye
            s = k - nt3(ls, (lh[c2], ll[c2]))
            s = jnp.where(tile >= PANELS, s, 0.0)
            if c2 == 0:
                s = jnp.where(tile_c == 0, l0, jnp.where(tile_c == 1, l1, s))
            for half in range(size // 128):
                stage[a, pl.ds(c2 * (size // 128) + half, size, stride=tile_cols * size // 128), :] = s[
                    :, half * 128 : half * 128 + 128
                ]
        writes.append(pltpu.make_async_copy(stage.at[a], out.at[a], osems.at[a]))
        writes[-1].start()
    writes.append(pltpu.make_async_copy(rest, solved, osems.at[tile_rows]))
    writes[-1].start()
    for copy in writes:
        copy.wait()


def per_device(points, rhs):
    rows_n = lax.axis_size("row")
    cols_n = lax.axis_size("col")
    tile_rows, _, size, feat = points.shape
    width = rhs.shape[-1]
    tile_cols = tile_rows * rows_n // cols_n
    pts = points[:, 0]
    right = rhs[:, 0].swapaxes(1, 2)
    jobs = 2 * PANELS + tile_cols
    hbm = pl.BlockSpec(memory_space=pltpu.HBM)
    piv_s, colp_s = (PANELS, size, feat), (tile_cols, size, feat)
    h_s, y_s = (3, 2, size, size), (width, PANELS * size)
    piv, colp, hs, ys = pl.pallas_call(
        functools.partial(factor_kernel, rows_n, cols_n, tile_cols),
        out_shape=(
            jax.ShapeDtypeStruct(piv_s, F32),
            jax.ShapeDtypeStruct(colp_s, F32),
            jax.ShapeDtypeStruct(h_s, BF16),
            jax.ShapeDtypeStruct(y_s, F32),
        ),
        in_specs=[hbm] * 2,
        out_specs=(hbm,) * 4,
        scratch_shapes=[
            pltpu.VMEM(piv_s, F32),
            pltpu.VMEM(colp_s, F32),
            pltpu.VMEM((PANELS, width, size), F32),
            pltpu.VMEM((size, size), F32),
            pltpu.VMEM((size, size), F32),
            pltpu.VMEM((size, size), F32),
            pltpu.VMEM(h_s, BF16),
            pltpu.VMEM(y_s, F32),
            pltpu.SemaphoreType.DMA((jobs, rows_n)),
            pltpu.SemaphoreType.DMA((jobs, 2)),
            pltpu.SemaphoreType.DMA((jobs,)),
            pltpu.SemaphoreType.DMA((4,)),
        ],
        compiler_params=pltpu.CompilerParams(
            collective_id=0, has_side_effects=True, vmem_limit_bytes=62 * 1024 * 1024
        ),
        name="factor",
    )(pts, right)
    out_s = (tile_rows, size * tile_cols * size // 128, 128)
    factored, solved = pl.pallas_call(
        functools.partial(tiles_kernel, rows_n, cols_n),
        out_shape=(
            jax.ShapeDtypeStruct(out_s, F32),
            jax.ShapeDtypeStruct((tile_rows, width, size), F32),
        ),
        in_specs=[hbm] * 6,
        out_specs=(hbm,) * 2,
        scratch_shapes=[
            pltpu.VMEM(pts.shape, F32),
            pltpu.VMEM(piv_s, F32),
            pltpu.VMEM(colp_s, F32),
            pltpu.VMEM(right.shape, F32),
            pltpu.VMEM(h_s, BF16),
            pltpu.VMEM(y_s, F32),
            pltpu.VMEM((tile_cols, size, PANELS * size), BF16),
            pltpu.VMEM((tile_cols, size, PANELS * size), BF16),
            pltpu.VMEM(out_s, F32),
            pltpu.VMEM((tile_rows, width, size), F32),
            pltpu.SemaphoreType.DMA((6,)),
            pltpu.SemaphoreType.DMA((tile_rows + 1,)),
        ],
        compiler_params=pltpu.CompilerParams(vmem_limit_bytes=62 * 1024 * 1024),
        name="tiles",
    )(pts, piv, colp, right, hs, ys)
    factored = factored.reshape(tile_rows, 1, size, tile_cols, 1, size)
    return factored, solved.swapaxes(1, 2)[:, None]


def solution(mesh):
    return jax.shard_map(
        per_device,
        mesh=mesh,
        in_specs=(P(None, "row", None, None), P(None, "row", None, "col")),
        out_specs=(P(None, "row", None, None, "col", None), P(None, "row", None, "col")),
        check_vma=False,
    )
```

```python
import functools

import jax
import jax.numpy as jnp
from jax import lax
from jax.experimental import pallas as pl
from jax.experimental.pallas import tpu as pltpu
from jax.sharding import PartitionSpec as P

PANELS = 2
SCALE = 3.0
NUGGET = 1.0
HIGHEST = lax.Precision.HIGHEST
MESH = pl.DeviceIdType.MESH
F32 = jnp.float32
BF16 = jnp.bfloat16
NB = 128
LOG2E = 1.4426950408889634


def split(x):
    hi = x.astype(BF16)
    return hi, (x - hi.astype(F32)).astype(BF16)


def nt(a, b):
    return lax.dot_general(a, b, (((1,), (1,)), ((), ())), preferred_element_type=F32)


def nt3(a, b):
    return nt(a[0], b[0]) + (nt(a[0], b[1]) + nt(a[1], b[0]))


def squared_exp(a, b, b_sq):
    a_sq = jnp.sum(a * a, axis=1, keepdims=True)
    inner = nt3(split(a), split(b))
    return jnp.exp((-SCALE / a.shape[1]) * (a_sq + b_sq - 2.0 * inner))


def row_squares(b):
    ones = jnp.ones((8, b.shape[1]), F32)
    return lax.dot_general(
        ones, b * b, (((1,), (1,)), ((), ())), precision=HIGHEST, preferred_element_type=F32
    )[:1]


def splat(tile, j):
    return jnp.broadcast_to(tile[:, j:j+1], tile.shape)
def rowof(tile, s):
    return jnp.broadcast_to(tile[s:s+1], tile.shape)

def base_inverse(block, width=16, ahead=2):
    lane = lax.broadcasted_iota(jnp.int32, (8, NB), 1)
    sub = lax.broadcasted_iota(jnp.int32, (8, NB), 0)
    v = [block[8 * q : 8 * q + 8] for q in range(NB // 8)]
    rows_n = len(v)
    per = width // 8
    out = []
    for j in range(0, NB, width):
        q0 = j // 8
        near = list(range(q0 + per, min(q0 + per + ahead, rows_n)))
        far = list(range(q0 + per + ahead, rows_n))
        d = [[splat(v[q0+t], j+n) for n in range(width)] for t in range(per)]
        d[0] = [jnp.where(lane >= 0, x, 0.0) for x in d[0]]
        low = [[splat(v[q], j+n) for n in range(width)] for q in near]
        inside = (lane >= j) & (lane < j+width)
        r = [jnp.where(inside, (lane - j == sub + 8*t).astype(F32), v[q0+t]) for t in range(per)]
        f = [None]*per
        S = [None]*width
        us = {}
        for n in range(0, width, 2):
            t, s = divmod(n, 8)
            a, b, c = rowof(d[t][n], s), rowof(d[t][n+1], s), rowof(d[t][n+1], s+1)
            det = a*c - b*b
            inv = 1.0/det
            ai, bi, ci = a*inv, b*inv, c*inv
            r0, r1 = rowof(r[t], s), rowof(r[t], s+1)
            rs = lax.rsqrt(a)
            f0 = r0*rs
            f1 = (a*r1 - b*r0)*(lax.rsqrt(det)*rs)
            f[t] = f0 if f[t] is None else jnp.where(sub == s, f0, f[t])
            f[t] = jnp.where(sub == s+1, f1, f[t])
            S[n], S[n+1] = ci*r0 - bi*r1, ai*r1 - bi*r0
            for m in range(n+2, width):
                x, y = rowof(d[t][m], s), rowof(d[t][m], s+1)
                u0, u1 = ci*x - bi*y, ai*y - bi*x
                us[n, m] = u0, u1
                for tt in range((n+2)//8, per):
                    d[tt][m] = d[tt][m] - (d[tt][n]*u0 + d[tt][n+1]*u1)
            for tt in range((n+2)//8, per):
                r[tt] = r[tt] - (d[tt][n]*S[n] + d[tt][n+1]*S[n+1])
        if near:
            for n in range(width-4, -1, -2):
                for m in range(width-1, n+1, -1):
                    u0, u1 = us[n, m]
                    S[n] = S[n] - u0*S[m]
                    S[n+1] = S[n+1] - u1*S[m]
        for t in range(per):
            out.append(jnp.where(lane <= j + 8*t + sub, f[t], 0.0))
        for i, q in enumerate(near):
            acc = [low[i][n]*S[n] for n in range(4)]
            for n in range(4, width):
                acc[n % 4] = acc[n % 4] + low[i][n]*S[n]
            v[q] = jnp.where(inside, 0.0, v[q]) - ((acc[0]+acc[1])+(acc[2]+acc[3]))
        if far:
            fc = jnp.concatenate(f, axis=0)
            hi = fc.astype(BF16)
            lo = (fc - hi.astype(F32)).astype(BF16)
            up = lax.dot_general(jnp.concatenate([hi, hi, lo], axis=0), jnp.concatenate([hi, lo, hi], axis=0),
                                 (((0,), (0,)), ((), ())), preferred_element_type=F32)
            for q in far:
                v[q] = jnp.where(inside, 0.0, v[q]) - up[8*q:8*q+8]
    return jnp.concatenate(out, axis=0)


def inverse_factor(w, h, inv):
    h[:NB, :NB] = inv
    h[:NB, NB:] = jnp.zeros((NB, w.shape[1] - NB), F32)
    first = split(inv)
    below = split(nt3(split(w[NB:, :NB]), first))
    w[NB:, NB:] = w[NB:, NB:] - nt3(below, below)
    mixed = split(nn3(below, first))
    inv = base_inverse(w[NB:, NB:])
    h[NB:, NB:] = inv
    h[NB:, :NB] = -nn3(split(inv), mixed)


def factor_kernel(
    rows_n, cols_n, tile_cols, pts, prhs, opiv, ocolp, oh, oy,
    piv, colp, rpiv, w, h0, h1, hs, ys, send, recv, local, wsem,
):
    row_id = lax.axis_index("row")
    col_id = lax.axis_index("col")
    stride = cols_n // rows_n

    barrier = pltpu.get_barrier_semaphore()
    for step in range(1, rows_n):
        other = lax.rem(row_id + step, rows_n)
        pl.semaphore_signal(barrier, inc=1, device_id={"row": other}, device_id_type=MESH)

    jobs = [(0, pts.at[0, pl.ds(n * NB, NB)], piv.at[0, pl.ds(n * NB, NB)]) for n in range(2)]
    jobs += [(k % rows_n, pts.at[k // rows_n], piv.at[k]) for k in range(1, PANELS)]
    jobs += [(k % rows_n, prhs.at[k // rows_n], rpiv.at[k]) for k in range(PANELS)]
    for c2 in range(tile_cols):
        slot = c2 * stride + col_id // rows_n
        jobs.append((lax.rem(col_id, rows_n), pts.at[slot], colp.at[c2]))

    chips = rows_n // 2
    chip, core = row_id // 2, lax.rem(row_id, 2)
    sibling = row_id + 1 - 2 * core

    def half_of(ref, half):
        height = ref.shape[0] // 2
        return ref.at[pl.ds(pl.multiple_of(half * height, height), height)]

    def remote(number, half, dest, slot, relay=False):
        _, src, dst = jobs[number]
        if number == 1:
            return pltpu.make_async_remote_copy(
                src_ref=src,
                dst_ref=dst,
                send_sem=send.at[number, slot],
                recv_sem=recv.at[number, 0],
                device_id={"row": dest},
                device_id_type=MESH,
            )
        return pltpu.make_async_remote_copy(
            src_ref=half_of(dst if relay else src, half),
            dst_ref=half_of(dst, half),
            send_sem=send.at[number, slot],
            recv_sem=recv.at[number, half],
            device_id={"row": dest},
            device_id_type=MESH,
        )

    def sends(number):
        out = []
        for step in range(1, chips):
            for half in range(2):
                dest = 2 * lax.rem(chip + step, chips) + half
                out.append(remote(number, half, dest, 2 * step + half))
        return out + [remote(number, half, sibling, half) for half in range(1 if number == 1 else 2)]

    def own(number):
        _, src, dst = jobs[number]
        return pltpu.make_async_copy(src, dst, local.at[number])

    def when(condition):
        return pl.when(condition)

    def launch(number):
        @when(row_id == jobs[number][0])
        def _():
            for copy in sends(number):
                copy.start()

    def relay(number):
        @when(chip != jobs[number][0] // 2)
        def _():
            copy = remote(number, core, sibling, 0, relay=True)
            copy.wait_recv()
            copy.start()

    def arrive(number):
        owner = jobs[number][0]

        @when(row_id == owner)
        def _():
            own(number).wait()

        @when(sibling == owner)
        def _():
            for half in range(2):
                remote(number, half, sibling, half).wait_recv()

        @when(chip != owner // 2)
        def _():
            remote(number, 1 - core, sibling, 0, relay=True).wait_recv()

    def drain(number):
        owner = jobs[number][0]

        @when(row_id == owner)
        def _():
            for copy in sends(number):
                copy.wait_send()

        @when(chip != owner // 2)
        def _():
            remote(number, core, sibling, 0, relay=True).wait_send()

    for number in range(len(jobs)):
        @when(row_id == jobs[number][0])
        def _(number=number):
            own(number).start()

    pl.semaphore_wait(barrier, rows_n - 1)
    launch(0)
    relay(0)
    arrive(0)
    drain(0)
    for number in range(1, len(jobs)):
        launch(number)

    size = piv.shape[1]
    eye = (
        lax.broadcasted_iota(jnp.int32, (size, size), 0) == lax.broadcasted_iota(jnp.int32, (size, size), 1)
    ).astype(F32)
    xa = piv[0, :NB]
    sqa = row_squares(xa)
    w[:NB, :NB] = squared_exp(xa, xa, sqa) + NUGGET * eye[:NB, :NB]
    inv = base_inverse(w[:NB, :NB])

    @when(row_id == 0)
    def _():
        own(1).wait()

    @when(row_id != 0)
    def _():
        remote(1, 0, 0, 0).wait_recv()

    xb = piv[0, NB:]
    w[NB:, :NB] = squared_exp(xb, xa, sqa)
    w[NB:, NB:] = squared_exp(xb, xb, row_squares(xb)) + NUGGET * eye[:NB, :NB]
    inverse_factor(w, h0, inv)
    x0 = piv[0]
    sq0 = row_squares(x0)
    h0s = split(h0[...])
    hs[:, : 3 * size] = right3(h0[...])

    for number in range(2, len(jobs)):
        relay(number)
    arrive(2)
    x1 = piv[1]
    sq1 = row_squares(x1)
    l10s = split(nt3(split(squared_exp(x1, x0, sq0)), h0s))
    w[...] = squared_exp(x1, x1, sq1) + NUGGET * eye - nt3(l10s, l10s)
    mixed = split(nn3(l10s, h0s))
    inverse_factor(w, h1, base_inverse(w[:NB, :NB]))

    for number in range(3, len(jobs)):
        arrive(number)
    writes = [pltpu.make_async_copy(piv, opiv, wsem.at[0]), pltpu.make_async_copy(colp, ocolp, wsem.at[1])]
    for copy in writes:
        copy.start()
    h1s = split(h1[...])
    hx = -nn3(h1s, mixed)
    hxs = split(hx)
    hs[:, 3 * size : 6 * size] = right3(hx)
    hs[:, 6 * size :] = right3(h1[...])
    writes.append(pltpu.make_async_copy(hs, oh, wsem.at[2]))
    writes[-1].start()
    r0, r1 = split(rpiv[0]), split(rpiv[1])
    ys[:, :size] = nt3(r0, h0s)
    ys[:, size:] = nt3(r0, hxs) + nt3(r1, h1s)
    writes.append(pltpu.make_async_copy(ys, oy, wsem.at[3]))
    writes[-1].start()
    @when(row_id == 0)
    def _():
        for copy in sends(1):
            copy.wait_send()

    for number in range(2, len(jobs)):
        drain(number)
    for copy in writes:
        copy.wait()


def nn(a, b):
    return lax.dot_general(a, b, (((1,), (0,)), ((), ())), preferred_element_type=F32)


def nn3(a, b):
    return nn(a[0], b[0]) + (nn(a[0], b[1]) + nn(a[1], b[0]))


def left3(x):
    hi, lo = split(x)
    return jnp.concatenate([hi, hi, lo], axis=1)


def right3(x):
    hi, lo = split(x)
    return jnp.concatenate([hi, lo, hi], axis=1)


def tiles_kernel(
    rows_n, cols_n, hpts, hpiv, hcolp, hrhs, hh, hy, out, solved,
    pts, piv, colp, rhs, hs, ys, k3, lr3, lc3, stage, rest, sems, osems,
):
    row_id = lax.axis_index("row")
    col_id = lax.axis_index("col")
    copies = [
        pltpu.make_async_copy(src, dst, sems.at[n])
        for n, (src, dst) in enumerate(
            ((hpiv, piv), (hpts, pts), (hcolp, colp), (hh, hs), (hrhs, rhs), (hy, ys))
        )
    ]
    for copy in copies:
        copy.start()
    tile_rows, size, feat = pts.shape
    tile_cols = colp.shape[0]
    high, wide = tile_rows * size, tile_cols * size
    scale = -SCALE / feat * LOG2E
    diagonal = lax.broadcasted_iota(jnp.int32, (size, size), 0) - lax.broadcasted_iota(
        jnp.int32, (size, size), 1
    )
    eye = (diagonal == 0).astype(F32)
    lower = diagonal >= 0

    def nugget(hit):
        return jnp.where(hit, NUGGET, 0.0) * eye

    def across(x):
        return right3(x * (-2.0 * scale)), row_squares(x) * scale

    def along(x):
        return left3(x), jnp.sum(x * x, axis=1, keepdims=True) * scale

    def covariance(a, b):
        return jnp.exp2((nt(a[0], b[0]) + a[1]) + b[1])

    for copy in copies[:3]:
        copy.wait()
    pivots = [across(piv[k]) for k in range(PANELS)]
    rows = along(pts[...].reshape(high, feat))
    xc = colp[...].reshape(wide, feat)
    cols = along(xc)
    for k in range(PANELS):
        for start, x, tile in ((0, rows, row_id), (high, cols, col_id)):
            value = covariance(x, pivots[k])
            top = left3(value[:size] + nugget(tile == k))
            k3[start : start + size, 3 * k * size : 3 * (k + 1) * size] = top
            k3[start + size : start + x[0].shape[0], 3 * k * size : 3 * (k + 1) * size] = left3(value[size:])

    copies[3].wait()
    for start, count, tile in ((high, wide, col_id), (0, high, row_id)):
        l0 = nt(k3[start : start + count, : 3 * size], hs[:, : 3 * size])
        l1 = nt(k3[start : start + count, :], hs[:, 3 * size :])
        for k, value in ((0, l0), (1, l1)):
            top = jnp.where((tile > k) | (lower & (tile == k)), value[:size], 0.0)
            for at, part in ((0, top), (size, value[size:])):
                hi, lo = split(part)
                span = pl.ds(at, part.shape[0])
                order = (hi, lo, hi) if start else (hi, hi, lo)
                for n, piece in enumerate(order):
                    place = pl.ds((PANELS * n + k) * size, size)
                    (lc3 if start else lr3)[span, place] = piece

    def put(a, c2, value):
        for half in range(size // 128):
            stage[a, pl.ds(c2 * (size // 128) + half, size, stride=wide // 128), :] = value[
                :, half * 128 : half * 128 + 128
            ]

    def schur(c2, begin, end):
        tile_c = c2 * cols_n + col_id
        value = covariance((rows[0][begin * size : end * size], rows[1][begin * size : end * size]), across(colp[c2]))
        value = value - nt(lr3[begin * size : end * size, :], lc3[c2 * size : (c2 + 1) * size, :])
        for a in range(begin, end):
            tile = a * rows_n + row_id
            part = value[(a - begin) * size : (a - begin + 1) * size] + nugget(tile == tile_c)
            put(a, c2, jnp.where(tile >= PANELS, part, 0.0) if a == 0 else part)

    @pl.when(col_id >= PANELS)
    def _():
        schur(0, 0, tile_rows)

    for k in range(PANELS):

        @pl.when(col_id == k)
        def _(k=k):
            for a in range(tile_rows):
                span = pl.ds(a * size, size)
                hi = lr3[span, k * size : (k + 1) * size].astype(F32)
                put(a, 0, hi + lr3[span, (2 * PANELS + k) * size : (2 * PANELS + k + 1) * size].astype(F32))

    for copy in copies[4:]:
        copy.wait()
    width = ys.shape[0]
    y = ys[...]
    filled = jnp.concatenate([y, jnp.zeros((128 - width, y.shape[1]), F32)], axis=0) if width < 128 else y
    update = nt(lr3[...], right3(filled))
    for a in range(tile_rows):
        tile = a * rows_n + row_id
        turned = jnp.concatenate(
            [update[a * size + n : a * size + n + 128].T[:width] for n in range(0, size, 128)], axis=1
        )
        value = rhs[a] - turned
        if a == 0:
            for k in range(PANELS):
                value = jnp.where(tile == k, y[:, k * size : (k + 1) * size], value)
        rest[a] = value
    writes = [pltpu.make_async_copy(rest, solved, osems.at[tile_rows])]
    writes[0].start()

    for c2 in range(1, tile_cols):
        for begin in range(0, tile_rows, 2):
            end = min(begin + 2, tile_rows)
            schur(c2, begin, end)
            if c2 == tile_cols - 1:
                for a in range(begin, end):
                    writes.append(pltpu.make_async_copy(stage.at[a], out.at[a], osems.at[a]))
                    writes[-1].start()
    for copy in writes:
        copy.wait()


def per_device(points, rhs):
    rows_n = lax.axis_size("row")
    cols_n = lax.axis_size("col")
    tile_rows, _, size, feat = points.shape
    width = rhs.shape[-1]
    tile_cols = tile_rows * rows_n // cols_n
    pts = points[:, 0]
    right = rhs[:, 0].swapaxes(1, 2)
    jobs = 2 * PANELS + tile_cols + 1
    hbm = pl.BlockSpec(memory_space=pltpu.HBM)
    piv_s, colp_s = (PANELS, size, feat), (tile_cols, size, feat)
    h_s, y_s = (size, 9 * size), (width, PANELS * size)
    piv, colp, hs, ys = pl.pallas_call(
        functools.partial(factor_kernel, rows_n, cols_n, tile_cols),
        out_shape=(
            jax.ShapeDtypeStruct(piv_s, F32),
            jax.ShapeDtypeStruct(colp_s, F32),
            jax.ShapeDtypeStruct(h_s, BF16),
            jax.ShapeDtypeStruct(y_s, F32),
        ),
        in_specs=[hbm] * 2,
        out_specs=(hbm,) * 4,
        scratch_shapes=[
            pltpu.VMEM(piv_s, F32),
            pltpu.VMEM(colp_s, F32),
            pltpu.VMEM((PANELS, width, size), F32),
            pltpu.VMEM((size, size), F32),
            pltpu.VMEM((size, size), F32),
            pltpu.VMEM((size, size), F32),
            pltpu.VMEM(h_s, BF16),
            pltpu.VMEM(y_s, F32),
            pltpu.SemaphoreType.DMA((jobs, rows_n)),
            pltpu.SemaphoreType.DMA((jobs, 2)),
            pltpu.SemaphoreType.DMA((jobs,)),
            pltpu.SemaphoreType.DMA((4,)),
        ],
        compiler_params=pltpu.CompilerParams(
            collective_id=0, has_side_effects=True, vmem_limit_bytes=62 * 1024 * 1024
        ),
        name="factor",
    )(pts, right)
    out_s = (tile_rows, size * tile_cols * size // 128, 128)
    factored, solved = pl.pallas_call(
        functools.partial(tiles_kernel, rows_n, cols_n),
        out_shape=(
            jax.ShapeDtypeStruct(out_s, F32),
            jax.ShapeDtypeStruct((tile_rows, width, size), F32),
        ),
        in_specs=[hbm] * 6,
        out_specs=(hbm,) * 2,
        scratch_shapes=[
            pltpu.VMEM(pts.shape, F32),
            pltpu.VMEM(piv_s, F32),
            pltpu.VMEM(colp_s, F32),
            pltpu.VMEM(right.shape, F32),
            pltpu.VMEM(h_s, BF16),
            pltpu.VMEM(y_s, F32),
            pltpu.VMEM(((tile_rows + tile_cols) * size, 3 * PANELS * size), BF16),
            pltpu.VMEM((tile_rows * size, 3 * PANELS * size), BF16),
            pltpu.VMEM((tile_cols * size, 3 * PANELS * size), BF16),
            pltpu.VMEM(out_s, F32),
            pltpu.VMEM((tile_rows, width, size), F32),
            pltpu.SemaphoreType.DMA((6,)),
            pltpu.SemaphoreType.DMA((tile_rows + 1,)),
        ],
        compiler_params=pltpu.CompilerParams(vmem_limit_bytes=62 * 1024 * 1024),
        name="tiles",
    )(pts, piv, colp, right, hs, ys)
    factored = factored.reshape(tile_rows, 1, size, tile_cols, 1, size)
    return factored, solved.swapaxes(1, 2)[:, None]


def solution(mesh):
    return jax.shard_map(
        per_device,
        mesh=mesh,
        in_specs=(P(None, "row", None, None), P(None, "row", None, "col")),
        out_specs=(P(None, "row", None, None, "col", None), P(None, "row", None, "col")),
        check_vma=False,
    )
```

```python
import functools

import jax
import jax.numpy as jnp
from jax import lax
from jax.experimental import pallas as pl
from jax.experimental.pallas import tpu as pltpu
from jax.sharding import PartitionSpec as P

PANELS = 2
SCALE = 3.0
NUGGET = 1.0
HIGHEST = lax.Precision.HIGHEST
MESH = pl.DeviceIdType.MESH
F32 = jnp.float32
BF16 = jnp.bfloat16
NB = 128
DIRECT = (1, 2)
LOG2E = 1.4426950408889634


def split(x):
    hi = x.astype(BF16)
    return hi, (x - hi.astype(F32)).astype(BF16)


def nt(a, b):
    return lax.dot_general(a, b, (((1,), (1,)), ((), ())), preferred_element_type=F32)


def nt3(a, b):
    return nt(a[0], b[0]) + (nt(a[0], b[1]) + nt(a[1], b[0]))


def squared_exp(a, b, b_sq):
    a_sq = jnp.sum(a * a, axis=1, keepdims=True)
    inner = nt3(split(a), split(b))
    return jnp.exp((-SCALE / a.shape[1]) * (a_sq + b_sq - 2.0 * inner))


def row_squares(b):
    ones = jnp.ones((8, b.shape[1]), F32)
    return lax.dot_general(
        ones, b * b, (((1,), (1,)), ((), ())), precision=HIGHEST, preferred_element_type=F32
    )[:1]


def splat(tile, j):
    return jnp.broadcast_to(tile[:, j:j+1], tile.shape)
def rowof(tile, s):
    return jnp.broadcast_to(tile[s:s+1], tile.shape)

def base_inverse(block, width=16, ahead=2):
    lane = lax.broadcasted_iota(jnp.int32, (8, NB), 1)
    sub = lax.broadcasted_iota(jnp.int32, (8, NB), 0)
    v = [block[8 * q : 8 * q + 8] for q in range(NB // 8)]
    rows_n = len(v)
    per = width // 8
    out = []
    for j in range(0, NB, width):
        q0 = j // 8
        near = list(range(q0 + per, min(q0 + per + ahead, rows_n)))
        far = list(range(q0 + per + ahead, rows_n))
        d = [[splat(v[q0+t], j+n) for n in range(width)] for t in range(per)]
        d[0] = [jnp.where(lane >= 0, x, 0.0) for x in d[0]]
        low = [[splat(v[q], j+n) for n in range(width)] for q in near]
        inside = (lane >= j) & (lane < j+width)
        r = [jnp.where(inside, (lane - j == sub + 8*t).astype(F32), v[q0+t]) for t in range(per)]
        f = [None]*per
        S = [None]*width
        us = {}
        for n in range(0, width, 2):
            t, s = divmod(n, 8)
            a, b, c = rowof(d[t][n], s), rowof(d[t][n+1], s), rowof(d[t][n+1], s+1)
            det = a*c - b*b
            inv = 1.0/det
            ai, bi, ci = a*inv, b*inv, c*inv
            r0, r1 = rowof(r[t], s), rowof(r[t], s+1)
            rs = lax.rsqrt(a)
            f0 = r0*rs
            f1 = (a*r1 - b*r0)*(lax.rsqrt(det)*rs)
            f[t] = f0 if f[t] is None else jnp.where(sub == s, f0, f[t])
            f[t] = jnp.where(sub == s+1, f1, f[t])
            S[n], S[n+1] = ci*r0 - bi*r1, ai*r1 - bi*r0
            for m in range(n+2, width):
                x, y = rowof(d[t][m], s), rowof(d[t][m], s+1)
                u0, u1 = ci*x - bi*y, ai*y - bi*x
                us[n, m] = u0, u1
                for tt in range((n+2)//8, per):
                    d[tt][m] = d[tt][m] - (d[tt][n]*u0 + d[tt][n+1]*u1)
            for tt in range((n+2)//8, per):
                r[tt] = r[tt] - (d[tt][n]*S[n] + d[tt][n+1]*S[n+1])
        if near:
            for n in range(width-4, -1, -2):
                for m in range(width-1, n+1, -1):
                    u0, u1 = us[n, m]
                    S[n] = S[n] - u0*S[m]
                    S[n+1] = S[n+1] - u1*S[m]
        for t in range(per):
            out.append(jnp.where(lane <= j + 8*t + sub, f[t], 0.0))
        for i, q in enumerate(near):
            acc = [low[i][n]*S[n] for n in range(4)]
            for n in range(4, width):
                acc[n % 4] = acc[n % 4] + low[i][n]*S[n]
            v[q] = jnp.where(inside, 0.0, v[q]) - ((acc[0]+acc[1])+(acc[2]+acc[3]))
        if far:
            fc = jnp.concatenate(f, axis=0)
            hi = fc.astype(BF16)
            lo = (fc - hi.astype(F32)).astype(BF16)
            up = lax.dot_general(jnp.concatenate([hi, hi, lo], axis=0), jnp.concatenate([hi, lo, hi], axis=0),
                                 (((0,), (0,)), ((), ())), preferred_element_type=F32)
            for q in far:
                v[q] = jnp.where(inside, 0.0, v[q]) - up[8*q:8*q+8]
    return jnp.concatenate(out, axis=0)


def inverse_factor(w, h, inv):
    h[:NB, :NB] = inv
    h[:NB, NB:] = jnp.zeros((NB, w.shape[1] - NB), F32)
    first = split(inv)
    below = split(nt3(split(w[NB:, :NB]), first))
    w[NB:, NB:] = w[NB:, NB:] - nt3(below, below)
    mixed = split(nn3(below, first))
    inv = base_inverse(w[NB:, NB:])
    h[NB:, NB:] = inv
    h[NB:, :NB] = -nn3(split(inv), mixed)


def factor_kernel(
    rows_n, cols_n, tile_cols, pts, prhs, opiv, ocolp, oh, orpiv,
    piv, colp, rpiv, w, h0, h1, hs, send, recv, local, wsem,
):
    row_id = lax.axis_index("row")
    col_id = lax.axis_index("col")
    stride = cols_n // rows_n

    barrier = pltpu.get_barrier_semaphore()
    for step in range(1, rows_n):
        other = lax.rem(row_id + step, rows_n)
        pl.semaphore_signal(barrier, inc=1, device_id={"row": other}, device_id_type=MESH)

    jobs = [(0, pts.at[0, pl.ds(n * NB, NB)], piv.at[0, pl.ds(n * NB, NB)]) for n in range(2)]
    jobs += [(k % rows_n, pts.at[k // rows_n], piv.at[k]) for k in range(1, PANELS)]
    jobs += [(k % rows_n, prhs.at[k // rows_n], rpiv.at[k]) for k in range(PANELS)]
    for c2 in range(tile_cols):
        slot = c2 * stride + col_id // rows_n
        jobs.append((lax.rem(col_id, rows_n), pts.at[slot], colp.at[c2]))

    chips = rows_n // 2
    chip, core = row_id // 2, lax.rem(row_id, 2)
    sibling = row_id + 1 - 2 * core

    def half_of(ref, half):
        height = ref.shape[0] // 2
        return ref.at[pl.ds(pl.multiple_of(half * height, height), height)]

    def remote(number, half, dest, slot, relay=False):
        _, src, dst = jobs[number]
        if number in DIRECT:
            return pltpu.make_async_remote_copy(
                src_ref=src,
                dst_ref=dst,
                send_sem=send.at[number, slot],
                recv_sem=recv.at[number, 0],
                device_id={"row": dest},
                device_id_type=MESH,
            )
        return pltpu.make_async_remote_copy(
            src_ref=half_of(dst if relay else src, half),
            dst_ref=half_of(dst, half),
            send_sem=send.at[number, slot],
            recv_sem=recv.at[number, half],
            device_id={"row": dest},
            device_id_type=MESH,
        )

    def sends(number):
        out = []
        for step in range(1, chips):
            for half in range(2):
                dest = 2 * lax.rem(chip + step, chips) + half
                out.append(remote(number, half, dest, 2 * step + half))
        return out + [remote(number, half, sibling, half) for half in range(1 if number in DIRECT else 2)]

    def own(number):
        _, src, dst = jobs[number]
        return pltpu.make_async_copy(src, dst, local.at[number])

    def when(condition):
        return pl.when(condition)

    def launch(number):
        @when(row_id == jobs[number][0])
        def _():
            for copy in sends(number):
                copy.start()

    def relay(number):
        @when(chip != jobs[number][0] // 2)
        def _():
            copy = remote(number, core, sibling, 0, relay=True)
            copy.wait_recv()
            copy.start()

    def arrive(number):
        owner = jobs[number][0]

        @when(row_id == owner)
        def _():
            own(number).wait()

        if number in DIRECT:
            @when(row_id != owner)
            def _():
                remote(number, 0, sibling, 0).wait_recv()
            return

        @when(sibling == owner)
        def _():
            for half in range(2):
                remote(number, half, sibling, half).wait_recv()

        @when(chip != owner // 2)
        def _():
            remote(number, 1 - core, sibling, 0, relay=True).wait_recv()

    def drain(number):
        owner = jobs[number][0]

        @when(row_id == owner)
        def _():
            for copy in sends(number):
                copy.wait_send()

        if number in DIRECT:
            return

        @when(chip != owner // 2)
        def _():
            remote(number, core, sibling, 0, relay=True).wait_send()

    for number in range(len(jobs)):
        @when(row_id == jobs[number][0])
        def _(number=number):
            own(number).start()

    pl.semaphore_wait(barrier, rows_n - 1)
    launch(0)
    relay(0)
    arrive(0)
    drain(0)
    for number in DIRECT:
        launch(number)

    size = piv.shape[1]
    eye = (
        lax.broadcasted_iota(jnp.int32, (size, size), 0) == lax.broadcasted_iota(jnp.int32, (size, size), 1)
    ).astype(F32)
    xa = piv[0, :NB]
    sqa = row_squares(xa)
    w[:NB, :NB] = squared_exp(xa, xa, sqa) + NUGGET * eye[:NB, :NB]
    inv = base_inverse(w[:NB, :NB])
    for number in range(3, len(jobs)):
        launch(number)
    arrive(1)
    xb = piv[0, NB:]
    w[NB:, :NB] = squared_exp(xb, xa, sqa)
    w[NB:, NB:] = squared_exp(xb, xb, row_squares(xb)) + NUGGET * eye[:NB, :NB]
    inverse_factor(w, h0, inv)
    x0 = piv[0]
    sq0 = row_squares(x0)
    h0s = split(h0[...])
    hs[0, 0], hs[0, 1] = h0s
    arrive(2)
    x1 = piv[1]
    sq1 = row_squares(x1)
    l10s = split(nt3(split(squared_exp(x1, x0, sq0)), h0s))
    w[...] = squared_exp(x1, x1, sq1) + NUGGET * eye - nt3(l10s, l10s)
    mixed = split(nn3(l10s, h0s))
    inv = base_inverse(w[:NB, :NB])
    for number in range(3, len(jobs)):
        relay(number)
    inverse_factor(w, h1, inv)
    for number in range(3, len(jobs)):
        arrive(number)
    writes = [
        pltpu.make_async_copy(src, dst, wsem.at[n]) for n, (src, dst) in enumerate(((piv, opiv), (colp, ocolp), (rpiv, orpiv)))
    ]
    for copy in writes:
        copy.start()
    h1s = split(h1[...])
    hs[1, 0], hs[1, 1] = h1s
    hs[2, 0], hs[2, 1] = split(-nn3(h1s, mixed))
    writes.append(pltpu.make_async_copy(hs, oh, wsem.at[3]))
    writes[-1].start()
    for number in range(1, len(jobs)):
        drain(number)
    for copy in writes:
        copy.wait()


def nn(a, b):
    return lax.dot_general(a, b, (((1,), (0,)), ((), ())), preferred_element_type=F32)


def nn3(a, b):
    return nn(a[0], b[0]) + (nn(a[0], b[1]) + nn(a[1], b[0]))


def left3(x):
    hi, lo = split(x)
    return jnp.concatenate([hi, hi, lo], axis=1)


def right3(x):
    hi, lo = split(x)
    return jnp.concatenate([hi, lo, hi], axis=1)


def tiles_kernel(
    rows_n, cols_n, hpts, hpiv, hcolp, hrhs, hh, hr, out, solved,
    pts, piv, colp, rhs, hs, rpiv, k3, lc3, stage, rest, sems, osems,
):
    row_id = lax.axis_index("row")
    col_id = lax.axis_index("col")
    copies = [
        pltpu.make_async_copy(src, dst, sems.at[n])
        for n, (src, dst) in enumerate(
            ((hpiv, piv), (hpts, pts), (hcolp, colp), (hh, hs), (hr, rpiv), (hrhs, rhs))
        )
    ]
    for copy in copies:
        copy.start()
    tile_rows, size, feat = pts.shape
    tile_cols = colp.shape[0]
    high, wide = tile_rows * size, tile_cols * size
    scale = -SCALE / feat * LOG2E
    diagonal = lax.broadcasted_iota(jnp.int32, (size, size), 0) - lax.broadcasted_iota(
        jnp.int32, (size, size), 1
    )
    eye = (diagonal == 0).astype(F32)
    lower = diagonal >= 0

    def nugget(hit):
        return jnp.where(hit, NUGGET, 0.0) * eye

    def across(x):
        return right3(x * (-2.0 * scale)), row_squares(x) * scale

    def along(x):
        return left3(x), jnp.sum(x * x, axis=1, keepdims=True) * scale

    def covariance(a, b):
        return jnp.exp2((nt(a[0], b[0]) + a[1]) + b[1])

    for copy in copies[:3]:
        copy.wait()
    pivots = [across(piv[k]) for k in range(PANELS)]
    xc = colp[...].reshape(wide, feat)

    def spread(ref, value, k, order):
        pieces = split(value)
        for n, which in enumerate(order):
            ref[:, pl.ds((PANELS * n + k) * size, size)] = pieces[which]

    def pivot_tiles(x, tile):
        side = along(x)
        values = []
        for k in range(PANELS):
            value = covariance(side, pivots[k])
            values.append(jnp.concatenate([value[:size] + nugget(tile == k), value[size:]], axis=0))
        return values

    kc = pivot_tiles(xc, col_id)
    copies[3].wait()
    copies[4].wait()
    width = rpiv.shape[1]
    padding = [jnp.zeros((-width % 16, size), F32)] if width % 16 else []
    kc = [split(jnp.concatenate([kc[k], rpiv[k]] + padding, axis=0)) for k in range(PANELS)]
    h0s, h1s, hxs = ((hs[n, 0], hs[n, 1]) for n in range(3))
    l0 = nt3(kc[0], h0s)
    l1 = nt3(kc[0], hxs) + nt3(kc[1], h1s)
    l0s, l1s = split(l0), split(l1)
    weighted = nn3(l0s, h0s) + nn3(l1s, hxs), nn3(l1s, h1s)
    for k in range(PANELS):
        spread(lc3, weighted[k][:wide], k, (0, 1, 0))
    ys = l0[wide : wide + width], l1[wide : wide + width]
    z = split(jnp.concatenate([value[wide : wide + width] for value in weighted], axis=1))
    xr = pts[...].reshape(high, feat)
    rows = along(xr)
    for k, value in enumerate(pivot_tiles(xr, row_id)):
        spread(k3, value, k, (0, 0, 1))

    def put(a, c2, value):
        for half in range(size // 128):
            stage[a, pl.ds(c2 * (size // 128) + half, size, stride=wide // 128), :] = value[
                :, half * 128 : half * 128 + 128
            ]

    def schur(c2, begin, end):
        tile_c = c2 * cols_n + col_id
        value = covariance((rows[0][begin * size : end * size], rows[1][begin * size : end * size]), across(colp[c2]))
        value = value - nt(k3[begin * size : end * size, :], lc3[c2 * size : (c2 + 1) * size, :])
        for a in range(begin, end):
            tile = a * rows_n + row_id
            part = value[(a - begin) * size : (a - begin + 1) * size] + nugget(tile == tile_c)
            put(a, c2, jnp.where(tile >= PANELS, part, 0.0) if a == 0 else part)

    @pl.when(col_id >= PANELS)
    def _():
        schur(0, 0, tile_rows)

    def panel(k):
        halves = [
            (k3[:, j * size : (j + 1) * size], k3[:, (2 * PANELS + j) * size : (2 * PANELS + j + 1) * size])
            for j in range(PANELS)
        ]
        value = nt3(halves[0], h0s) if k == 0 else nt3(halves[0], hxs) + nt3(halves[1], h1s)
        top = jnp.where((row_id > k) | (lower & (row_id == k)), value[:size], 0.0)
        for a in range(tile_rows):
            put(a, 0, value[a * size : (a + 1) * size] if a else top)

    for k in range(PANELS):

        @pl.when(col_id == k)
        def _(k=k):
            panel(k)

    copies[5].wait()
    z = [piece.astype(F32) for piece in z]
    room = max(NB, 2 * width)
    filled = jnp.concatenate(
        [jnp.concatenate([piece, piece], axis=1) for piece in z]
        + ([jnp.zeros((room - 2 * width, 2 * PANELS * size), F32)] if room > 2 * width else []),
        axis=0,
    ).astype(BF16)
    update = nt(k3[:, PANELS * size :], filled)
    for a in range(tile_rows):
        tile = a * rows_n + row_id
        turned = jnp.concatenate(
            [update[a * size + n : a * size + n + 128].T for n in range(0, size, 128)], axis=1
        )
        value = rhs[a] - (turned[:width] + turned[width : 2 * width])
        if a == 0:
            for k in range(PANELS):
                value = jnp.where(tile == k, ys[k], value)
        rest[a] = value
    writes = [pltpu.make_async_copy(rest, solved, osems.at[tile_rows])]
    writes[0].start()

    for c2 in range(1, tile_cols):
        for begin in range(0, tile_rows, 2):
            end = min(begin + 2, tile_rows)
            schur(c2, begin, end)
            if c2 == tile_cols - 1:
                for a in range(begin, end):
                    writes.append(pltpu.make_async_copy(stage.at[a], out.at[a], osems.at[a]))
                    writes[-1].start()
    for copy in writes:
        copy.wait()


def per_device(points, rhs):
    rows_n = lax.axis_size("row")
    cols_n = lax.axis_size("col")
    tile_rows, _, size, feat = points.shape
    width = rhs.shape[-1]
    tile_cols = tile_rows * rows_n // cols_n
    pts = points[:, 0]
    right = rhs[:, 0].swapaxes(1, 2)
    jobs = 2 * PANELS + tile_cols + 1
    hbm = pl.BlockSpec(memory_space=pltpu.HBM)
    piv_s, colp_s = (PANELS, size, feat), (tile_cols, size, feat)
    h_s, r_s = (3, 2, size, size), (PANELS, width, size)
    piv, colp, hs, rpiv = pl.pallas_call(
        functools.partial(factor_kernel, rows_n, cols_n, tile_cols),
        out_shape=(
            jax.ShapeDtypeStruct(piv_s, F32),
            jax.ShapeDtypeStruct(colp_s, F32),
            jax.ShapeDtypeStruct(h_s, BF16),
            jax.ShapeDtypeStruct(r_s, F32),
        ),
        in_specs=[hbm] * 2,
        out_specs=(hbm,) * 4,
        scratch_shapes=[
            pltpu.VMEM(piv_s, F32),
            pltpu.VMEM(colp_s, F32),
            pltpu.VMEM(r_s, F32),
            pltpu.VMEM((size, size), F32),
            pltpu.VMEM((size, size), F32),
            pltpu.VMEM((size, size), F32),
            pltpu.VMEM(h_s, BF16),
            pltpu.SemaphoreType.DMA((jobs, rows_n)),
            pltpu.SemaphoreType.DMA((jobs, 2)),
            pltpu.SemaphoreType.DMA((jobs,)),
            pltpu.SemaphoreType.DMA((4,)),
        ],
        compiler_params=pltpu.CompilerParams(
            collective_id=0, has_side_effects=True, vmem_limit_bytes=62 * 1024 * 1024
        ),
        name="factor",
    )(pts, right)
    out_s = (tile_rows, size * tile_cols * size // 128, 128)
    factored, solved = pl.pallas_call(
        functools.partial(tiles_kernel, rows_n, cols_n),
        out_shape=(
            jax.ShapeDtypeStruct(out_s, F32),
            jax.ShapeDtypeStruct((tile_rows, width, size), F32),
        ),
        in_specs=[hbm] * 6,
        out_specs=(hbm,) * 2,
        scratch_shapes=[
            pltpu.VMEM(pts.shape, F32),
            pltpu.VMEM(piv_s, F32),
            pltpu.VMEM(colp_s, F32),
            pltpu.VMEM(right.shape, F32),
            pltpu.VMEM(h_s, BF16),
            pltpu.VMEM(r_s, F32),
            pltpu.VMEM((tile_rows * size, 3 * PANELS * size), BF16),
            pltpu.VMEM((tile_cols * size, 3 * PANELS * size), BF16),
            pltpu.VMEM(out_s, F32),
            pltpu.VMEM((tile_rows, width, size), F32),
            pltpu.SemaphoreType.DMA((6,)),
            pltpu.SemaphoreType.DMA((tile_rows + 1,)),
        ],
        compiler_params=pltpu.CompilerParams(vmem_limit_bytes=62 * 1024 * 1024),
        name="tiles",
    )(pts, piv, colp, right, hs, rpiv)
    factored = factored.reshape(tile_rows, 1, size, tile_cols, 1, size)
    return factored, solved.swapaxes(1, 2)[:, None]


def solution(mesh):
    return jax.shard_map(
        per_device,
        mesh=mesh,
        in_specs=(P(None, "row", None, None), P(None, "row", None, "col")),
        out_specs=(P(None, "row", None, None, "col", None), P(None, "row", None, "col")),
        check_vma=False,
    )
```

```python
import functools

import jax
import jax.numpy as jnp
from jax import lax
from jax.experimental import pallas as pl
from jax.experimental.pallas import tpu as pltpu
from jax.sharding import PartitionSpec as P

PANELS = 2
SCALE = 3.0
NUGGET = 1.0
HIGHEST = lax.Precision.HIGHEST
MESH = pl.DeviceIdType.MESH
F32 = jnp.float32
BF16 = jnp.bfloat16
NB = 128
DIRECT = (1, 2)
LOG2E = 1.4426950408889634


def split(x):
    hi = x.astype(BF16)
    return hi, (x - hi.astype(F32)).astype(BF16)


def nt(a, b):
    return lax.dot_general(a, b, (((1,), (1,)), ((), ())), preferred_element_type=F32)


def nt3(a, b):
    return nt(a[0], b[0]) + (nt(a[0], b[1]) + nt(a[1], b[0]))


def squared_exp(a, b, b_sq):
    a_sq = jnp.sum(a * a, axis=1, keepdims=True)
    inner = nt3(split(a), split(b))
    return jnp.exp((-SCALE / a.shape[1]) * (a_sq + b_sq - 2.0 * inner))


def row_squares(b):
    ones = jnp.ones((8, b.shape[1]), F32)
    return lax.dot_general(
        ones, b * b, (((1,), (1,)), ((), ())), precision=HIGHEST, preferred_element_type=F32
    )[:1]


def splat(tile, j):
    return jnp.broadcast_to(tile[:, j:j+1], tile.shape)
def rowof(tile, s):
    return jnp.broadcast_to(tile[s:s+1], tile.shape)

def base_inverse(block, fill=None, width=16, ahead=2):
    lane = lax.broadcasted_iota(jnp.int32, (8, NB), 1)
    sub = lax.broadcasted_iota(jnp.int32, (8, NB), 0)
    v = [block[8 * q : 8 * q + 8] for q in range(NB // 8)]
    rows_n = len(v)
    per = width // 8
    out = []
    for j in range(0, NB, width):
        q0 = j // 8
        near = list(range(q0 + per, min(q0 + per + ahead, rows_n)))
        far = list(range(q0 + per + ahead, rows_n))
        d = [[splat(v[q0+t], j+n) for n in range(width)] for t in range(per)]
        d[0] = [jnp.where(lane >= 0, x, 0.0) for x in d[0]]
        low = [[splat(v[q], j+n) for n in range(width)] for q in near]
        inside = (lane >= j) & (lane < j+width)
        if fill is not None:
            fill(j // width)
        r = [jnp.where(inside, (lane - j == sub + 8*t).astype(F32), v[q0+t]) for t in range(per)]
        f = [None]*per
        S = [None]*width
        us = {}
        for n in range(0, width, 2):
            t, s = divmod(n, 8)
            a, b, c = rowof(d[t][n], s), rowof(d[t][n+1], s), rowof(d[t][n+1], s+1)
            det = a*c - b*b
            inv = 1.0/det
            ai, bi, ci = a*inv, b*inv, c*inv
            r0, r1 = rowof(r[t], s), rowof(r[t], s+1)
            rs = lax.rsqrt(a)
            f0 = r0*rs
            f1 = (a*r1 - b*r0)*(lax.rsqrt(det)*rs)
            f[t] = f0 if f[t] is None else jnp.where(sub == s, f0, f[t])
            f[t] = jnp.where(sub == s+1, f1, f[t])
            S[n], S[n+1] = ci*r0 - bi*r1, ai*r1 - bi*r0
            for m in range(n+2, width):
                x, y = rowof(d[t][m], s), rowof(d[t][m], s+1)
                u0, u1 = ci*x - bi*y, ai*y - bi*x
                us[n, m] = u0, u1
                for tt in range((n+2)//8, per):
                    d[tt][m] = d[tt][m] - (d[tt][n]*u0 + d[tt][n+1]*u1)
            for tt in range((n+2)//8, per):
                r[tt] = r[tt] - (d[tt][n]*S[n] + d[tt][n+1]*S[n+1])
        if near:
            for n in range(width-4, -1, -2):
                for m in range(width-1, n+1, -1):
                    u0, u1 = us[n, m]
                    S[n] = S[n] - u0*S[m]
                    S[n+1] = S[n+1] - u1*S[m]
        for t in range(per):
            out.append(jnp.where(lane <= j + 8*t + sub, f[t], 0.0))
        for i, q in enumerate(near):
            acc = [low[i][n]*S[n] for n in range(4)]
            for n in range(4, width):
                acc[n % 4] = acc[n % 4] + low[i][n]*S[n]
            v[q] = jnp.where(inside, 0.0, v[q]) - ((acc[0]+acc[1])+(acc[2]+acc[3]))
        if far:
            fc = jnp.concatenate(f, axis=0)
            hi = fc.astype(BF16)
            lo = (fc - hi.astype(F32)).astype(BF16)
            up = lax.dot_general(jnp.concatenate([hi, hi, lo], axis=0), jnp.concatenate([hi, lo, hi], axis=0),
                                 (((0,), (0,)), ((), ())), preferred_element_type=F32)
            for q in far:
                v[q] = jnp.where(inside, 0.0, v[q]) - up[8*q:8*q+8]
    return jnp.concatenate(out, axis=0)


def inverse_factor(w, h, inv, fill=None):
    h[:NB, :NB] = inv
    h[:NB, NB:] = jnp.zeros((NB, w.shape[1] - NB), F32)
    first = split(inv)
    below = split(nt3(split(w[NB:, :NB]), first))
    w[NB:, NB:] = w[NB:, NB:] - nt3(below, below)
    mixed = split(nn3(below, first))
    inv = base_inverse(w[NB:, NB:], fill)
    h[NB:, NB:] = inv
    h[NB:, :NB] = -nn3(split(inv), mixed)


def factor_kernel(
    rows_n, cols_n, tile_cols, pts, prhs, opiv, ocolp, oh, orpiv, ok2, ol3, osq,
    piv, colp, rpiv, w, h0, h1, hs, own_pts, k2, l3, sq, send, recv, local, wsem,
):
    row_id = lax.axis_index("row")
    col_id = lax.axis_index("col")
    stride = cols_n // rows_n

    barrier = pltpu.get_barrier_semaphore()
    for step in range(1, rows_n):
        other = lax.rem(row_id + step, rows_n)
        pl.semaphore_signal(barrier, inc=1, device_id={"row": other}, device_id_type=MESH)

    jobs = [(0, pts.at[0, pl.ds(n * NB, NB)], piv.at[0, pl.ds(n * NB, NB)]) for n in range(2)]
    jobs += [(k % rows_n, pts.at[k // rows_n], piv.at[k]) for k in range(1, PANELS)]
    jobs += [(k % rows_n, prhs.at[k // rows_n], rpiv.at[k]) for k in range(PANELS)]
    for c2 in range(tile_cols):
        slot = c2 * stride + col_id // rows_n
        jobs.append((lax.rem(col_id, rows_n), pts.at[slot], colp.at[c2]))

    chips = rows_n // 2
    chip, core = row_id // 2, lax.rem(row_id, 2)
    sibling = row_id + 1 - 2 * core

    def half_of(ref, half):
        height = ref.shape[0] // 2
        return ref.at[pl.ds(pl.multiple_of(half * height, height), height)]

    def remote(number, half, dest, slot, relay=False):
        _, src, dst = jobs[number]
        if number in DIRECT:
            return pltpu.make_async_remote_copy(
                src_ref=src,
                dst_ref=dst,
                send_sem=send.at[number, slot],
                recv_sem=recv.at[number, 0],
                device_id={"row": dest},
                device_id_type=MESH,
            )
        return pltpu.make_async_remote_copy(
            src_ref=half_of(dst if relay else src, half),
            dst_ref=half_of(dst, half),
            send_sem=send.at[number, slot],
            recv_sem=recv.at[number, half],
            device_id={"row": dest},
            device_id_type=MESH,
        )

    def sends(number):
        out = []
        for step in range(1, chips):
            for half in range(2):
                dest = 2 * lax.rem(chip + step, chips) + half
                out.append(remote(number, half, dest, 2 * step + half))
        return out + [remote(number, half, sibling, half) for half in range(1 if number in DIRECT else 2)]

    def own(number):
        _, src, dst = jobs[number]
        return pltpu.make_async_copy(src, dst, local.at[number])

    def when(condition):
        return pl.when(condition)

    def launch(number):
        @when(row_id == jobs[number][0])
        def _():
            for copy in sends(number):
                copy.start()

    def relay(number):
        @when(chip != jobs[number][0] // 2)
        def _():
            copy = remote(number, core, sibling, 0, relay=True)
            copy.wait_recv()
            copy.start()

    def arrive(number):
        owner = jobs[number][0]

        @when(row_id == owner)
        def _():
            own(number).wait()

        if number in DIRECT:
            @when(row_id != owner)
            def _():
                remote(number, 0, sibling, 0).wait_recv()
            return

        @when(sibling == owner)
        def _():
            for half in range(2):
                remote(number, half, sibling, half).wait_recv()

        @when(chip != owner // 2)
        def _():
            remote(number, 1 - core, sibling, 0, relay=True).wait_recv()

    def drain(number):
        owner = jobs[number][0]

        @when(row_id == owner)
        def _():
            for copy in sends(number):
                copy.wait_send()

        if number in DIRECT:
            return

        @when(chip != owner // 2)
        def _():
            remote(number, core, sibling, 0, relay=True).wait_send()

    for number in range(len(jobs)):
        @when(row_id == jobs[number][0])
        def _(number=number):
            own(number).start()

    rows_copy = pltpu.make_async_copy(pts, own_pts, wsem.at[5])
    rows_copy.start()
    pl.semaphore_wait(barrier, rows_n - 1)
    launch(0)
    rows_copy.wait()
    side = along(own_pts[...].reshape(l3.shape[0], own_pts.shape[2]))
    l3[...] = side[0]
    sq[...] = jnp.broadcast_to(side[1], sq.shape)
    early = [pltpu.make_async_copy(l3, ol3, wsem.at[6]), pltpu.make_async_copy(sq, osq, wsem.at[7])]
    for copy in early:
        copy.start()
    relay(0)
    arrive(0)
    drain(0)
    for number in DIRECT:
        launch(number)

    size = piv.shape[1]
    eye = (
        lax.broadcasted_iota(jnp.int32, (size, size), 0) == lax.broadcasted_iota(jnp.int32, (size, size), 1)
    ).astype(F32)

    def row_tiles(k):
        b = across(piv[k])
        step = own_pts.shape[0] * size * 16 // NB

        def piece(n):
            span = pl.ds(n * step, step)
            value = covariance((l3[span, :], widen(sq[span, :], size)), b)
            if n * step < size:
                value = value + jnp.where(row_id == k, NUGGET, 0.0) * eye[n * step : (n + 1) * step]
            hi, lo = split(value)
            k2[span, pl.ds(k * size, size)] = hi
            k2[span, pl.ds((PANELS + k) * size, size)] = lo

        return piece

    xa = piv[0, :NB]
    sqa = row_squares(xa)
    w[:NB, :NB] = squared_exp(xa, xa, sqa) + NUGGET * eye[:NB, :NB]
    inv = base_inverse(w[:NB, :NB])
    for number in range(3, len(jobs)):
        launch(number)
    arrive(1)
    xb = piv[0, NB:]
    w[NB:, :NB] = squared_exp(xb, xa, sqa)
    w[NB:, NB:] = squared_exp(xb, xb, row_squares(xb)) + NUGGET * eye[:NB, :NB]
    x0 = piv[0]
    sq0 = row_squares(x0)
    inverse_factor(w, h0, inv, row_tiles(0))
    h0s = split(h0[...])
    hs[0, 0], hs[0, 1] = h0s
    arrive(2)
    x1 = piv[1]
    sq1 = row_squares(x1)
    l10s = split(nt3(split(squared_exp(x1, x0, sq0)), h0s))
    w[...] = squared_exp(x1, x1, sq1) + NUGGET * eye - nt3(l10s, l10s)
    mixed = split(nn3(l10s, h0s))
    inv = base_inverse(w[:NB, :NB], row_tiles(1))
    writes = [pltpu.make_async_copy(k2, ok2, wsem.at[4])]
    writes[0].start()
    for number in range(3, len(jobs)):
        relay(number)
    inverse_factor(w, h1, inv)
    for number in range(3, len(jobs)):
        arrive(number)
    writes += early + [
        pltpu.make_async_copy(src, dst, wsem.at[n]) for n, (src, dst) in enumerate(((piv, opiv), (colp, ocolp), (rpiv, orpiv)))
    ]
    for copy in writes[3:]:
        copy.start()
    h1s = split(h1[...])
    hs[1, 0], hs[1, 1] = h1s
    hs[2, 0], hs[2, 1] = split(-nn3(h1s, mixed))
    writes.append(pltpu.make_async_copy(hs, oh, wsem.at[3]))
    writes[-1].start()
    for number in range(1, len(jobs)):
        drain(number)
    for copy in writes:
        copy.wait()


def nn(a, b):
    return lax.dot_general(a, b, (((1,), (0,)), ((), ())), preferred_element_type=F32)


def nn3(a, b):
    return nn(a[0], b[0]) + (nn(a[0], b[1]) + nn(a[1], b[0]))


def scale_of(feat):
    return -SCALE / feat * LOG2E


def across(x):
    scale = scale_of(x.shape[1])
    return right3(x * (-2.0 * scale)), row_squares(x) * scale


def along(x):
    return left3(x), jnp.sum(x * x, axis=1, keepdims=True) * scale_of(x.shape[1])


def covariance(a, b):
    return jnp.exp2((nt(a[0], b[0]) + a[1]) + b[1])


def widen(x, size):
    return jnp.concatenate([x] * (size // x.shape[1]), axis=1)


def left3(x):
    hi, lo = split(x)
    return jnp.concatenate([hi, hi, lo], axis=1)


def right3(x):
    hi, lo = split(x)
    return jnp.concatenate([hi, lo, hi], axis=1)


def tiles_kernel(
    rows_n, cols_n, hpts, hpiv, hcolp, hrhs, hh, hr, hk2, hsq, out, solved,
    pts, sq, piv, colp, rhs, hs, rpiv, k2, lc3, stage, rest, sems, osems,
):
    row_id = lax.axis_index("row")
    col_id = lax.axis_index("col")
    copies = [
        pltpu.make_async_copy(src, dst, sems.at[n])
        for n, (src, dst) in enumerate(
            ((hpiv, piv), (hcolp, colp), (hpts, pts), (hh, hs), (hr, rpiv), (hk2, k2), (hrhs, rhs), (hsq, sq))
        )
    ]
    for copy in copies:
        copy.start()
    tile_cols, size, feat = colp.shape
    tile_rows = pts.shape[0] // size
    high, wide = tile_rows * size, tile_cols * size
    diagonal = lax.broadcasted_iota(jnp.int32, (size, size), 0) - lax.broadcasted_iota(
        jnp.int32, (size, size), 1
    )
    eye = (diagonal == 0).astype(F32)
    lower = diagonal >= 0

    def nugget(hit):
        return jnp.where(hit, NUGGET, 0.0) * eye

    for copy in copies[:2]:
        copy.wait()
    pivots = [across(piv[k]) for k in range(PANELS)]
    xc = colp[...].reshape(wide, feat)

    def spread(ref, value, k, order):
        pieces = split(value)
        for n, which in enumerate(order):
            ref[:, pl.ds((PANELS * n + k) * size, size)] = pieces[which]

    def pivot_tiles(x, tile):
        side = along(x)
        values = []
        for k in range(PANELS):
            value = covariance(side, pivots[k])
            values.append(jnp.concatenate([value[:size] + nugget(tile == k), value[size:]], axis=0))
        return values

    kc = pivot_tiles(xc, col_id)
    copies[3].wait()
    copies[4].wait()
    width = rpiv.shape[1]
    padding = [jnp.zeros((-width % 16, size), F32)] if width % 16 else []
    kc = [split(jnp.concatenate([kc[k], rpiv[k]] + padding, axis=0)) for k in range(PANELS)]
    h0s, h1s, hxs = ((hs[n, 0], hs[n, 1]) for n in range(3))
    l0 = nt3(kc[0], h0s)
    l1 = nt3(kc[0], hxs) + nt3(kc[1], h1s)
    l0s, l1s = split(l0), split(l1)
    weighted = nn3(l0s, h0s) + nn3(l1s, hxs), nn3(l1s, h1s)
    for k in range(PANELS):
        spread(lc3, weighted[k][:wide], k, (0, 1, 0))
    ys = l0[wide : wide + width], l1[wide : wide + width]
    z = split(jnp.concatenate([value[wide : wide + width] for value in weighted], axis=1))
    copies[2].wait()
    copies[7].wait()
    copies[5].wait()

    def stacked(begin, end):
        span = pl.ds(begin * size, (end - begin) * size)
        return jnp.concatenate([k2[span, : PANELS * size], k2[span, :]], axis=1)

    def put(a, c2, value):
        for half in range(size // 128):
            stage[a, pl.ds(c2 * (size // 128) + half, size, stride=wide // 128), :] = value[
                :, half * 128 : half * 128 + 128
            ]

    def schur(c2, begin, end):
        tile_c = c2 * cols_n + col_id
        value = covariance((pts[begin * size : end * size, :], widen(sq[begin * size : end * size, :], size)), across(colp[c2]))
        value = value - nt(stacked(begin, end), lc3[c2 * size : (c2 + 1) * size, :])
        for a in range(begin, end):
            tile = a * rows_n + row_id
            part = value[(a - begin) * size : (a - begin + 1) * size] + nugget(tile == tile_c)
            put(a, c2, jnp.where(tile >= PANELS, part, 0.0) if a == 0 else part)

    @pl.when(col_id >= PANELS)
    def _():
        schur(0, 0, tile_rows)

    def panel(k):
        halves = [
            (k2[:, j * size : (j + 1) * size], k2[:, (PANELS + j) * size : (PANELS + j + 1) * size])
            for j in range(PANELS)
        ]
        value = nt3(halves[0], h0s) if k == 0 else nt3(halves[0], hxs) + nt3(halves[1], h1s)
        top = jnp.where((row_id > k) | (lower & (row_id == k)), value[:size], 0.0)
        for a in range(tile_rows):
            put(a, 0, value[a * size : (a + 1) * size] if a else top)

    for k in range(PANELS):

        @pl.when(col_id == k)
        def _(k=k):
            panel(k)

    copies[6].wait()
    z = [piece.astype(F32) for piece in z]
    room = max(NB, 2 * width)
    filled = jnp.concatenate(
        [jnp.concatenate([piece, piece], axis=1) for piece in z]
        + ([jnp.zeros((room - 2 * width, 2 * PANELS * size), F32)] if room > 2 * width else []),
        axis=0,
    ).astype(BF16)
    update = nt(k2[...], filled)
    for a in range(tile_rows):
        tile = a * rows_n + row_id
        turned = jnp.concatenate(
            [update[a * size + n : a * size + n + 128].T for n in range(0, size, 128)], axis=1
        )
        value = rhs[a] - (turned[:width] + turned[width : 2 * width])
        if a == 0:
            for k in range(PANELS):
                value = jnp.where(tile == k, ys[k], value)
        rest[a] = value
    writes = [pltpu.make_async_copy(rest, solved, osems.at[tile_rows])]
    writes[0].start()

    for c2 in range(1, tile_cols):
        for begin in range(0, tile_rows, 2):
            end = min(begin + 2, tile_rows)
            schur(c2, begin, end)
            if c2 == tile_cols - 1:
                for a in range(begin, end):
                    writes.append(pltpu.make_async_copy(stage.at[a], out.at[a], osems.at[a]))
                    writes[-1].start()
    for copy in writes:
        copy.wait()


def per_device(points, rhs):
    rows_n = lax.axis_size("row")
    cols_n = lax.axis_size("col")
    tile_rows, _, size, feat = points.shape
    width = rhs.shape[-1]
    tile_cols = tile_rows * rows_n // cols_n
    pts = points[:, 0]
    right = rhs[:, 0].swapaxes(1, 2)
    jobs = 2 * PANELS + tile_cols + 1
    hbm = pl.BlockSpec(memory_space=pltpu.HBM)
    piv_s, colp_s = (PANELS, size, feat), (tile_cols, size, feat)
    h_s, r_s = (3, 2, size, size), (PANELS, width, size)
    k_s = (tile_rows * size, 2 * PANELS * size)
    l_s, q_s = (tile_rows * size, 3 * feat), (tile_rows * size, 128)
    piv, colp, hs, rpiv, k2, l3, sq = pl.pallas_call(
        functools.partial(factor_kernel, rows_n, cols_n, tile_cols),
        out_shape=(
            jax.ShapeDtypeStruct(piv_s, F32),
            jax.ShapeDtypeStruct(colp_s, F32),
            jax.ShapeDtypeStruct(h_s, BF16),
            jax.ShapeDtypeStruct(r_s, F32),
            jax.ShapeDtypeStruct(k_s, BF16),
            jax.ShapeDtypeStruct(l_s, BF16),
            jax.ShapeDtypeStruct(q_s, F32),
        ),
        in_specs=[hbm] * 2,
        out_specs=(hbm,) * 7,
        scratch_shapes=[
            pltpu.VMEM(piv_s, F32),
            pltpu.VMEM(colp_s, F32),
            pltpu.VMEM(r_s, F32),
            pltpu.VMEM((size, size), F32),
            pltpu.VMEM((size, size), F32),
            pltpu.VMEM((size, size), F32),
            pltpu.VMEM(h_s, BF16),
            pltpu.VMEM(pts.shape, F32),
            pltpu.VMEM(k_s, BF16),
            pltpu.VMEM(l_s, BF16),
            pltpu.VMEM(q_s, F32),
            pltpu.SemaphoreType.DMA((jobs, rows_n)),
            pltpu.SemaphoreType.DMA((jobs, 2)),
            pltpu.SemaphoreType.DMA((jobs,)),
            pltpu.SemaphoreType.DMA((8,)),
        ],
        compiler_params=pltpu.CompilerParams(
            collective_id=0, has_side_effects=True, vmem_limit_bytes=62 * 1024 * 1024
        ),
        name="factor",
    )(pts, right)
    out_s = (tile_rows, size * tile_cols * size // 128, 128)
    factored, solved = pl.pallas_call(
        functools.partial(tiles_kernel, rows_n, cols_n),
        out_shape=(
            jax.ShapeDtypeStruct(out_s, F32),
            jax.ShapeDtypeStruct((tile_rows, width, size), F32),
        ),
        in_specs=[hbm] * 8,
        out_specs=(hbm,) * 2,
        scratch_shapes=[
            pltpu.VMEM(l_s, BF16),
            pltpu.VMEM(q_s, F32),
            pltpu.VMEM(piv_s, F32),
            pltpu.VMEM(colp_s, F32),
            pltpu.VMEM(right.shape, F32),
            pltpu.VMEM(h_s, BF16),
            pltpu.VMEM(r_s, F32),
            pltpu.VMEM(k_s, BF16),
            pltpu.VMEM((tile_cols * size, 3 * PANELS * size), BF16),
            pltpu.VMEM(out_s, F32),
            pltpu.VMEM((tile_rows, width, size), F32),
            pltpu.SemaphoreType.DMA((8,)),
            pltpu.SemaphoreType.DMA((tile_rows + 1,)),
        ],
        compiler_params=pltpu.CompilerParams(vmem_limit_bytes=62 * 1024 * 1024),
        name="tiles",
    )(l3, piv, colp, right, hs, rpiv, k2, sq)
    factored = factored.reshape(tile_rows, 1, size, tile_cols, 1, size)
    return factored, solved.swapaxes(1, 2)[:, None]


def solution(mesh):
    return jax.shard_map(
        per_device,
        mesh=mesh,
        in_specs=(P(None, "row", None, None), P(None, "row", None, "col")),
        out_specs=(P(None, "row", None, None, "col", None), P(None, "row", None, "col")),
        check_vma=False,
    )
```

```python
import functools

import jax
import jax.numpy as jnp
from jax import lax
from jax.experimental import pallas as pl
from jax.experimental.pallas import tpu as pltpu
from jax.sharding import PartitionSpec as P

PANELS = 2
SCALE = 3.0
NUGGET = 1.0
HIGHEST = lax.Precision.HIGHEST
MESH = pl.DeviceIdType.MESH
F32 = jnp.float32
BF16 = jnp.bfloat16
NB = 128
DIRECT = (1, 2)
LOG2E = 1.4426950408889634


def split(x):
    hi = x.astype(BF16)
    return hi, (x - hi.astype(F32)).astype(BF16)


def nt(a, b):
    return lax.dot_general(a, b, (((1,), (1,)), ((), ())), preferred_element_type=F32)


def nt3(a, b):
    return nt(a[0], b[0]) + (nt(a[0], b[1]) + nt(a[1], b[0]))


def squared_exp(a, b, b_sq):
    a_sq = jnp.sum(a * a, axis=1, keepdims=True)
    inner = nt3(split(a), split(b))
    return jnp.exp((-SCALE / a.shape[1]) * (a_sq + b_sq - 2.0 * inner))


def row_squares(b):
    ones = jnp.ones((8, b.shape[1]), F32)
    return lax.dot_general(
        ones, b * b, (((1,), (1,)), ((), ())), precision=HIGHEST, preferred_element_type=F32
    )[:1]


def splat(tile, j):
    return jnp.broadcast_to(tile[:, j:j+1], tile.shape)
def rowof(tile, s):
    return jnp.broadcast_to(tile[s:s+1], tile.shape)

def base_inverse(block, fill=None, width=16, ahead=2):
    lane = lax.broadcasted_iota(jnp.int32, (8, NB), 1)
    sub = lax.broadcasted_iota(jnp.int32, (8, NB), 0)
    v = [block[8 * q : 8 * q + 8] for q in range(NB // 8)]
    rows_n = len(v)
    per = width // 8
    out = []
    for j in range(0, NB, width):
        q0 = j // 8
        near = list(range(q0 + per, min(q0 + per + ahead, rows_n)))
        far = list(range(q0 + per + ahead, rows_n))
        d = [[splat(v[q0+t], j+n) for n in range(width)] for t in range(per)]
        d[0] = [jnp.where(lane >= 0, x, 0.0) for x in d[0]]
        low = [[splat(v[q], j+n) for n in range(width)] for q in near]
        inside = (lane >= j) & (lane < j+width)
        if fill is not None:
            fill(j // width)
        r = [jnp.where(inside, (lane - j == sub + 8*t).astype(F32), v[q0+t]) for t in range(per)]
        f = [None]*per
        S = [None]*width
        us = {}
        for n in range(0, width, 2):
            t, s = divmod(n, 8)
            a, b, c = rowof(d[t][n], s), rowof(d[t][n+1], s), rowof(d[t][n+1], s+1)
            det = a*c - b*b
            inv = 1.0/det
            ai, bi, ci = a*inv, b*inv, c*inv
            r0, r1 = rowof(r[t], s), rowof(r[t], s+1)
            rs = lax.rsqrt(a)
            f0 = r0*rs
            f1 = (a*r1 - b*r0)*(lax.rsqrt(det)*rs)
            f[t] = f0 if f[t] is None else jnp.where(sub == s, f0, f[t])
            f[t] = jnp.where(sub == s+1, f1, f[t])
            S[n], S[n+1] = ci*r0 - bi*r1, ai*r1 - bi*r0
            for m in range(n+2, width):
                x, y = rowof(d[t][m], s), rowof(d[t][m], s+1)
                u0, u1 = ci*x - bi*y, ai*y - bi*x
                us[n, m] = u0, u1
                for tt in range((n+2)//8, per):
                    d[tt][m] = d[tt][m] - (d[tt][n]*u0 + d[tt][n+1]*u1)
            for tt in range((n+2)//8, per):
                r[tt] = r[tt] - (d[tt][n]*S[n] + d[tt][n+1]*S[n+1])
        if near:
            for n in range(width-4, -1, -2):
                for m in range(width-1, n+1, -1):
                    u0, u1 = us[n, m]
                    S[n] = S[n] - u0*S[m]
                    S[n+1] = S[n+1] - u1*S[m]
        for t in range(per):
            out.append(jnp.where(lane <= j + 8*t + sub, f[t], 0.0))
        for i, q in enumerate(near):
            acc = [low[i][n]*S[n] for n in range(4)]
            for n in range(4, width):
                acc[n % 4] = acc[n % 4] + low[i][n]*S[n]
            v[q] = jnp.where(inside, 0.0, v[q]) - ((acc[0]+acc[1])+(acc[2]+acc[3]))
        if far:
            fc = jnp.concatenate(f, axis=0)
            hi = fc.astype(BF16)
            lo = (fc - hi.astype(F32)).astype(BF16)
            up = lax.dot_general(jnp.concatenate([hi, hi, lo], axis=0), jnp.concatenate([hi, lo, hi], axis=0),
                                 (((0,), (0,)), ((), ())), preferred_element_type=F32)
            for q in far:
                v[q] = jnp.where(inside, 0.0, v[q]) - up[8*q:8*q+8]
    return jnp.concatenate(out, axis=0)


def inverse_factor(w, h, inv, fill=None):
    h[:NB, :NB] = inv
    h[:NB, NB:] = jnp.zeros((NB, w.shape[1] - NB), F32)
    first = split(inv)
    below = split(nt3(split(w[NB:, :NB]), first))
    w[NB:, NB:] = w[NB:, NB:] - nt3(below, below)
    mixed = split(nn3(below, first))
    inv = base_inverse(w[NB:, NB:], fill)
    h[NB:, NB:] = inv
    h[NB:, :NB] = -nn3(split(inv), mixed)


def factor_kernel(
    rows_n, cols_n, tile_cols, pts, prhs, opiv, ocolp, oh, orpiv, ok2, ol3, osq,
    piv, colp, rpiv, w, h0, h1, hs, own_pts, k2, l3, sq, send, recv, local, wsem,
):
    row_id = lax.axis_index("row")
    col_id = lax.axis_index("col")
    stride = cols_n // rows_n

    barrier = pltpu.get_barrier_semaphore()
    for step in range(1, rows_n):
        other = lax.rem(row_id + step, rows_n)
        pl.semaphore_signal(barrier, inc=1, device_id={"row": other}, device_id_type=MESH)

    jobs = [(0, pts.at[0, pl.ds(n * NB, NB)], piv.at[0, pl.ds(n * NB, NB)]) for n in range(2)]
    jobs += [(k % rows_n, pts.at[k // rows_n], piv.at[k]) for k in range(1, PANELS)]
    jobs += [(k % rows_n, prhs.at[k // rows_n], rpiv.at[k]) for k in range(PANELS)]
    for c2 in range(tile_cols):
        slot = c2 * stride + col_id // rows_n
        jobs.append((lax.rem(col_id, rows_n), pts.at[slot], colp.at[c2]))

    chips = rows_n // 2
    chip, core = row_id // 2, lax.rem(row_id, 2)
    sibling = row_id + 1 - 2 * core

    def half_of(ref, half):
        height = ref.shape[0] // 2
        return ref.at[pl.ds(pl.multiple_of(half * height, height), height)]

    def remote(number, half, dest, slot, relay=False):
        _, src, dst = jobs[number]
        if number in DIRECT:
            return pltpu.make_async_remote_copy(
                src_ref=src,
                dst_ref=dst,
                send_sem=send.at[number, slot],
                recv_sem=recv.at[number, 0],
                device_id={"row": dest},
                device_id_type=MESH,
            )
        return pltpu.make_async_remote_copy(
            src_ref=half_of(dst if relay else src, half),
            dst_ref=half_of(dst, half),
            send_sem=send.at[number, slot],
            recv_sem=recv.at[number, half],
            device_id={"row": dest},
            device_id_type=MESH,
        )

    def sends(number):
        out = []
        for step in range(1, chips):
            for half in (1, 0):
                dest = 2 * lax.rem(chip + step, chips) + half
                out.append(remote(number, half, dest, 2 * step + half))
        return out + [remote(number, half, sibling, half) for half in range(1 if number in DIRECT else 2)]

    def own(number):
        _, src, dst = jobs[number]
        return pltpu.make_async_copy(src, dst, local.at[number])

    def when(condition):
        return pl.when(condition)

    def launch(number):
        @when(row_id == jobs[number][0])
        def _():
            for copy in sends(number):
                copy.start()

    def relay(number):
        @when(chip != jobs[number][0] // 2)
        def _():
            copy = remote(number, core, sibling, 0, relay=True)
            copy.wait_recv()
            copy.start()

    def arrive(number):
        owner = jobs[number][0]

        @when(row_id == owner)
        def _():
            own(number).wait()

        if number in DIRECT:
            @when(row_id != owner)
            def _():
                remote(number, 0, sibling, 0).wait_recv()
            return

        @when(sibling == owner)
        def _():
            for half in range(2):
                remote(number, half, sibling, half).wait_recv()

        @when(chip != owner // 2)
        def _():
            remote(number, 1 - core, sibling, 0, relay=True).wait_recv()

    def drain(number):
        owner = jobs[number][0]

        @when(row_id == owner)
        def _():
            for copy in sends(number):
                copy.wait_send()

        if number in DIRECT:
            return

        @when(chip != owner // 2)
        def _():
            remote(number, core, sibling, 0, relay=True).wait_send()

    for number in range(len(jobs)):
        @when(row_id == jobs[number][0])
        def _(number=number):
            own(number).start()

    rows_copy = pltpu.make_async_copy(pts, own_pts, wsem.at[5])
    rows_copy.start()
    pl.semaphore_wait(barrier, rows_n - 1)
    launch(0)
    rows_copy.wait()
    side = along(own_pts[...].reshape(l3.shape[0], own_pts.shape[2]))
    l3[...] = side[0]
    sq[...] = jnp.broadcast_to(side[1], sq.shape)
    early = [pltpu.make_async_copy(l3, ol3, wsem.at[6]), pltpu.make_async_copy(sq, osq, wsem.at[7])]
    for copy in early:
        copy.start()
    relay(0)
    arrive(0)
    drain(0)
    for number in DIRECT:
        launch(number)

    size = piv.shape[1]
    eye = (
        lax.broadcasted_iota(jnp.int32, (size, size), 0) == lax.broadcasted_iota(jnp.int32, (size, size), 1)
    ).astype(F32)

    def row_tiles(k):
        b = across(piv[k])
        step = own_pts.shape[0] * size * 16 // NB

        def piece(n):
            span = pl.ds(n * step, step)
            value = covariance((l3[span, :], widen(sq[span, :], size)), b)
            if n * step < size:
                value = value + jnp.where(row_id == k, NUGGET, 0.0) * eye[n * step : (n + 1) * step]
            hi, lo = split(value)
            k2[span, pl.ds(k * size, size)] = hi
            k2[span, pl.ds((PANELS + k) * size, size)] = lo

        return piece

    xa = piv[0, :NB]
    sqa = row_squares(xa)
    w[:NB, :NB] = squared_exp(xa, xa, sqa) + NUGGET * eye[:NB, :NB]
    inv = base_inverse(w[:NB, :NB])
    for number in range(3, len(jobs)):
        launch(number)
    arrive(1)
    xb = piv[0, NB:]
    w[NB:, :NB] = squared_exp(xb, xa, sqa)
    w[NB:, NB:] = squared_exp(xb, xb, row_squares(xb)) + NUGGET * eye[:NB, :NB]
    x0 = piv[0]
    sq0 = row_squares(x0)
    inverse_factor(w, h0, inv, row_tiles(0))
    h0s = split(h0[...])
    hs[0, 0], hs[0, 1] = h0s
    arrive(2)
    x1 = piv[1]
    sq1 = row_squares(x1)
    l10s = split(nt3(split(squared_exp(x1, x0, sq0)), h0s))
    w[...] = squared_exp(x1, x1, sq1) + NUGGET * eye - nt3(l10s, l10s)
    mixed = split(nn3(l10s, h0s))
    inv = base_inverse(w[:NB, :NB], row_tiles(1))
    writes = [pltpu.make_async_copy(k2, ok2, wsem.at[4])]
    writes[0].start()
    for number in range(3, len(jobs)):
        relay(number)
    inverse_factor(w, h1, inv)
    for number in range(3, len(jobs)):
        arrive(number)
    writes += early + [
        pltpu.make_async_copy(src, dst, wsem.at[n]) for n, (src, dst) in enumerate(((piv, opiv), (colp, ocolp), (rpiv, orpiv)))
    ]
    for copy in writes[3:]:
        copy.start()
    h1s = split(h1[...])
    hs[1, 0], hs[1, 1] = h1s
    hs[2, 0], hs[2, 1] = split(-nn3(h1s, mixed))
    writes.append(pltpu.make_async_copy(hs, oh, wsem.at[3]))
    writes[-1].start()
    for number in range(1, len(jobs)):
        drain(number)
    for copy in writes:
        copy.wait()


def nn(a, b):
    return lax.dot_general(a, b, (((1,), (0,)), ((), ())), preferred_element_type=F32)


def nn3(a, b):
    return nn(a[0], b[0]) + (nn(a[0], b[1]) + nn(a[1], b[0]))


def scale_of(feat):
    return -SCALE / feat * LOG2E


def across(x):
    scale = scale_of(x.shape[1])
    return right3(x * (-2.0 * scale)), row_squares(x) * scale


def along(x):
    return left3(x), jnp.sum(x * x, axis=1, keepdims=True) * scale_of(x.shape[1])


def covariance(a, b):
    return jnp.exp2((nt(a[0], b[0]) + a[1]) + b[1])


def widen(x, size):
    return jnp.concatenate([x] * (size // x.shape[1]), axis=1)


def left3(x):
    hi, lo = split(x)
    return jnp.concatenate([hi, hi, lo], axis=1)


def right3(x):
    hi, lo = split(x)
    return jnp.concatenate([hi, lo, hi], axis=1)


def tiles_kernel(
    rows_n, cols_n, hpts, hpiv, hcolp, hrhs, hh, hr, hk2, hsq, out, solved,
    pts, sq, piv, colp, rhs, hs, rpiv, k2, lc3, stage, rest, sems, osems,
):
    row_id = lax.axis_index("row")
    col_id = lax.axis_index("col")
    copies = [
        pltpu.make_async_copy(src, dst, sems.at[n])
        for n, (src, dst) in enumerate(
            ((hpiv, piv), (hcolp, colp), (hpts, pts), (hh, hs), (hr, rpiv), (hk2, k2), (hrhs, rhs), (hsq, sq))
        )
    ]
    for copy in copies:
        copy.start()
    tile_cols, size, feat = colp.shape
    tile_rows = pts.shape[0] // size
    high, wide = tile_rows * size, tile_cols * size
    diagonal = lax.broadcasted_iota(jnp.int32, (size, size), 0) - lax.broadcasted_iota(
        jnp.int32, (size, size), 1
    )
    eye = (diagonal == 0).astype(F32)
    lower = diagonal >= 0

    def nugget(hit):
        return jnp.where(hit, NUGGET, 0.0) * eye

    for copy in copies[:2]:
        copy.wait()
    pivots = [across(piv[k]) for k in range(PANELS)]
    xc = colp[...].reshape(wide, feat)

    def spread(ref, value, k, order):
        pieces = split(value)
        for n, which in enumerate(order):
            ref[:, pl.ds((PANELS * n + k) * size, size)] = pieces[which]

    def pivot_tiles(x, tile):
        side = along(x)
        values = []
        for k in range(PANELS):
            value = covariance(side, pivots[k])
            values.append(jnp.concatenate([value[:size] + nugget(tile == k), value[size:]], axis=0))
        return values

    kc = pivot_tiles(xc, col_id)
    copies[3].wait()
    copies[4].wait()
    width = rpiv.shape[1]
    padding = [jnp.zeros((-width % 16, size), F32)] if width % 16 else []
    kc = [split(jnp.concatenate([kc[k], rpiv[k]] + padding, axis=0)) for k in range(PANELS)]
    h0s, h1s, hxs = ((hs[n, 0], hs[n, 1]) for n in range(3))
    l0 = nt3(kc[0], h0s)
    l1 = nt3(kc[0], hxs) + nt3(kc[1], h1s)
    l0s, l1s = split(l0), split(l1)
    weighted = nn3(l0s, h0s) + nn3(l1s, hxs), nn3(l1s, h1s)
    for k in range(PANELS):
        spread(lc3, weighted[k][:wide], k, (0, 1, 0))
    ys = l0[wide : wide + width], l1[wide : wide + width]
    z = split(jnp.concatenate([value[wide : wide + width] for value in weighted], axis=1))
    copies[2].wait()
    copies[7].wait()
    copies[5].wait()

    def stacked(begin, end):
        span = pl.ds(begin * size, (end - begin) * size)
        return jnp.concatenate([k2[span, : PANELS * size], k2[span, :]], axis=1)

    def put(a, c2, value):
        for half in range(size // 128):
            stage[a, pl.ds(c2 * (size // 128) + half, size, stride=wide // 128), :] = value[
                :, half * 128 : half * 128 + 128
            ]

    def schur(c2, begin, end):
        tile_c = c2 * cols_n + col_id
        value = covariance((pts[begin * size : end * size, :], widen(sq[begin * size : end * size, :], size)), across(colp[c2]))
        value = value - nt(stacked(begin, end), lc3[c2 * size : (c2 + 1) * size, :])
        for a in range(begin, end):
            tile = a * rows_n + row_id
            part = value[(a - begin) * size : (a - begin + 1) * size] + nugget(tile == tile_c)
            put(a, c2, jnp.where(tile >= PANELS, part, 0.0) if a == 0 else part)

    @pl.when(col_id >= PANELS)
    def _():
        schur(0, 0, tile_rows)

    def panel(k):
        halves = [
            (k2[:, j * size : (j + 1) * size], k2[:, (PANELS + j) * size : (PANELS + j + 1) * size])
            for j in range(PANELS)
        ]
        value = nt3(halves[0], h0s) if k == 0 else nt3(halves[0], hxs) + nt3(halves[1], h1s)
        top = jnp.where((row_id > k) | (lower & (row_id == k)), value[:size], 0.0)
        for a in range(tile_rows):
            put(a, 0, value[a * size : (a + 1) * size] if a else top)

    for k in range(PANELS):

        @pl.when(col_id == k)
        def _(k=k):
            panel(k)

    copies[6].wait()
    z = [piece.astype(F32) for piece in z]
    room = max(NB, 2 * width)
    filled = jnp.concatenate(
        [jnp.concatenate([piece, piece], axis=1) for piece in z]
        + ([jnp.zeros((room - 2 * width, 2 * PANELS * size), F32)] if room > 2 * width else []),
        axis=0,
    ).astype(BF16)
    update = nt(k2[...], filled)
    for a in range(tile_rows):
        tile = a * rows_n + row_id
        turned = jnp.concatenate(
            [update[a * size + n : a * size + n + 128].T for n in range(0, size, 128)], axis=1
        )
        value = rhs[a] - (turned[:width] + turned[width : 2 * width])
        if a == 0:
            for k in range(PANELS):
                value = jnp.where(tile == k, ys[k], value)
        rest[a] = value
    writes = [pltpu.make_async_copy(rest, solved, osems.at[tile_rows])]
    writes[0].start()

    for c2 in range(1, tile_cols):
        for begin in range(0, tile_rows, 2):
            end = min(begin + 2, tile_rows)
            schur(c2, begin, end)
            if c2 == tile_cols - 1:
                for a in range(begin, end):
                    writes.append(pltpu.make_async_copy(stage.at[a], out.at[a], osems.at[a]))
                    writes[-1].start()
    for copy in writes:
        copy.wait()


def per_device(points, rhs):
    rows_n = lax.axis_size("row")
    cols_n = lax.axis_size("col")
    tile_rows, _, size, feat = points.shape
    width = rhs.shape[-1]
    tile_cols = tile_rows * rows_n // cols_n
    pts = points[:, 0]
    right = rhs[:, 0].swapaxes(1, 2)
    jobs = 2 * PANELS + tile_cols + 1
    hbm = pl.BlockSpec(memory_space=pltpu.HBM)
    piv_s, colp_s = (PANELS, size, feat), (tile_cols, size, feat)
    h_s, r_s = (3, 2, size, size), (PANELS, width, size)
    k_s = (tile_rows * size, 2 * PANELS * size)
    l_s, q_s = (tile_rows * size, 3 * feat), (tile_rows * size, 128)
    piv, colp, hs, rpiv, k2, l3, sq = pl.pallas_call(
        functools.partial(factor_kernel, rows_n, cols_n, tile_cols),
        out_shape=(
            jax.ShapeDtypeStruct(piv_s, F32),
            jax.ShapeDtypeStruct(colp_s, F32),
            jax.ShapeDtypeStruct(h_s, BF16),
            jax.ShapeDtypeStruct(r_s, F32),
            jax.ShapeDtypeStruct(k_s, BF16),
            jax.ShapeDtypeStruct(l_s, BF16),
            jax.ShapeDtypeStruct(q_s, F32),
        ),
        in_specs=[hbm] * 2,
        out_specs=(hbm,) * 7,
        scratch_shapes=[
            pltpu.VMEM(piv_s, F32),
            pltpu.VMEM(colp_s, F32),
            pltpu.VMEM(r_s, F32),
            pltpu.VMEM((size, size), F32),
            pltpu.VMEM((size, size), F32),
            pltpu.VMEM((size, size), F32),
            pltpu.VMEM(h_s, BF16),
            pltpu.VMEM(pts.shape, F32),
            pltpu.VMEM(k_s, BF16),
            pltpu.VMEM(l_s, BF16),
            pltpu.VMEM(q_s, F32),
            pltpu.SemaphoreType.DMA((jobs, rows_n)),
            pltpu.SemaphoreType.DMA((jobs, 2)),
            pltpu.SemaphoreType.DMA((jobs,)),
            pltpu.SemaphoreType.DMA((8,)),
        ],
        compiler_params=pltpu.CompilerParams(
            collective_id=0, has_side_effects=True, vmem_limit_bytes=62 * 1024 * 1024
        ),
        name="factor",
    )(pts, right)
    out_s = (tile_rows, size * tile_cols * size // 128, 128)
    factored, solved = pl.pallas_call(
        functools.partial(tiles_kernel, rows_n, cols_n),
        out_shape=(
            jax.ShapeDtypeStruct(out_s, F32),
            jax.ShapeDtypeStruct((tile_rows, width, size), F32),
        ),
        in_specs=[hbm] * 8,
        out_specs=(hbm,) * 2,
        scratch_shapes=[
            pltpu.VMEM(l_s, BF16),
            pltpu.VMEM(q_s, F32),
            pltpu.VMEM(piv_s, F32),
            pltpu.VMEM(colp_s, F32),
            pltpu.VMEM(right.shape, F32),
            pltpu.VMEM(h_s, BF16),
            pltpu.VMEM(r_s, F32),
            pltpu.VMEM(k_s, BF16),
            pltpu.VMEM((tile_cols * size, 3 * PANELS * size), BF16),
            pltpu.VMEM(out_s, F32),
            pltpu.VMEM((tile_rows, width, size), F32),
            pltpu.SemaphoreType.DMA((8,)),
            pltpu.SemaphoreType.DMA((tile_rows + 1,)),
        ],
        compiler_params=pltpu.CompilerParams(vmem_limit_bytes=62 * 1024 * 1024),
        name="tiles",
    )(l3, piv, colp, right, hs, rpiv, k2, sq)
    factored = factored.reshape(tile_rows, 1, size, tile_cols, 1, size)
    return factored, solved.swapaxes(1, 2)[:, None]


def solution(mesh):
    return jax.shard_map(
        per_device,
        mesh=mesh,
        in_specs=(P(None, "row", None, None), P(None, "row", None, "col")),
        out_specs=(P(None, "row", None, None, "col", None), P(None, "row", None, "col")),
        check_vma=False,
    )
```

```python
import functools

import jax
import jax.numpy as jnp
from jax import lax
from jax.experimental import pallas as pl
from jax.experimental.pallas import tpu as pltpu
from jax.sharding import PartitionSpec as P

PANELS = 2
SCALE = 3.0
NUGGET = 1.0
HIGHEST = lax.Precision.HIGHEST
MESH = pl.DeviceIdType.MESH
F32 = jnp.float32
BF16 = jnp.bfloat16
NB = 128
DIRECT = (1, 2)
LOG2E = 1.4426950408889634


def split(x):
    hi = x.astype(BF16)
    return hi, (x - hi.astype(F32)).astype(BF16)


def nt(a, b):
    return lax.dot_general(a, b, (((1,), (1,)), ((), ())), preferred_element_type=F32)


def nt3(a, b):
    return nt(a[0], b[0]) + (nt(a[0], b[1]) + nt(a[1], b[0]))


def squared_exp(a, b, b_sq):
    scale = scale_of(a.shape[1])
    side = along(a)
    return jnp.exp2((nt(side[0], right3(b * (-2.0 * scale))) + side[1]) + b_sq * scale)


def row_squares(b):
    ones = jnp.ones((8, b.shape[1]), F32)
    return lax.dot_general(
        ones, b * b, (((1,), (1,)), ((), ())), precision=HIGHEST, preferred_element_type=F32
    )[:1]


def splat(tile, j):
    return jnp.broadcast_to(tile[:, j:j+1], tile.shape)
def rowof(tile, s):
    return jnp.broadcast_to(tile[s:s+1], tile.shape)

def base_inverse(block, fill=None, width=16, ahead=2):
    lane = lax.broadcasted_iota(jnp.int32, (8, NB), 1)
    sub = lax.broadcasted_iota(jnp.int32, (8, NB), 0)
    v = [block[8 * q : 8 * q + 8] for q in range(NB // 8)]
    rows_n = len(v)
    per = width // 8
    out = []
    for j in range(0, NB, width):
        q0 = j // 8
        near = list(range(q0 + per, min(q0 + per + ahead, rows_n)))
        far = list(range(q0 + per + ahead, rows_n))
        d = [[splat(v[q0+t], j+n) for n in range(width)] for t in range(per)]
        d[0] = [jnp.where(lane >= 0, x, 0.0) for x in d[0]]
        low = [[splat(v[q], j+n) for n in range(width)] for q in near]
        inside = (lane >= j) & (lane < j+width)
        if fill is not None:
            fill(j // width)
        r = [jnp.where(inside, (lane - j == sub + 8*t).astype(F32), v[q0+t]) for t in range(per)]
        f = [None]*per
        S = [None]*width
        us = {}
        for n in range(0, width, 2):
            t, s = divmod(n, 8)
            a, b, c = rowof(d[t][n], s), rowof(d[t][n+1], s), rowof(d[t][n+1], s+1)
            det = a*c - b*b
            inv = 1.0/det
            ai, bi, ci = a*inv, b*inv, c*inv
            r0, r1 = rowof(r[t], s), rowof(r[t], s+1)
            rs = lax.rsqrt(a)
            f0 = r0*rs
            f1 = (a*r1 - b*r0)*(lax.rsqrt(det)*rs)
            f[t] = f0 if f[t] is None else jnp.where(sub == s, f0, f[t])
            f[t] = jnp.where(sub == s+1, f1, f[t])
            S[n], S[n+1] = ci*r0 - bi*r1, ai*r1 - bi*r0
            for m in range(n+2, width):
                x, y = rowof(d[t][m], s), rowof(d[t][m], s+1)
                u0, u1 = ci*x - bi*y, ai*y - bi*x
                us[n, m] = u0, u1
                for tt in range((n+2)//8, per):
                    d[tt][m] = d[tt][m] - (d[tt][n]*u0 + d[tt][n+1]*u1)
            for tt in range((n+2)//8, per):
                r[tt] = r[tt] - (d[tt][n]*S[n] + d[tt][n+1]*S[n+1])
        if near:
            for n in range(width-4, -1, -2):
                for m in range(width-1, n+1, -1):
                    u0, u1 = us[n, m]
                    S[n] = S[n] - u0*S[m]
                    S[n+1] = S[n+1] - u1*S[m]
        for t in range(per):
            out.append(jnp.where(lane <= j + 8*t + sub, f[t], 0.0))
        for i, q in enumerate(near):
            acc = [low[i][n]*S[n] for n in range(4)]
            for n in range(4, width):
                acc[n % 4] = acc[n % 4] + low[i][n]*S[n]
            v[q] = jnp.where(inside, 0.0, v[q]) - ((acc[0]+acc[1])+(acc[2]+acc[3]))
        if far:
            fc = jnp.concatenate(f, axis=0)
            hi = fc.astype(BF16)
            lo = (fc - hi.astype(F32)).astype(BF16)
            up = lax.dot_general(jnp.concatenate([hi, hi, lo], axis=0), jnp.concatenate([hi, lo, hi], axis=0),
                                 (((0,), (0,)), ((), ())), preferred_element_type=F32)
            for q in far:
                v[q] = jnp.where(inside, 0.0, v[q]) - up[8*q:8*q+8]
    return jnp.concatenate(out, axis=0)


def inverse_factor(w, h, inv, fill=None):
    h[:NB, :NB] = inv
    h[:NB, NB:] = jnp.zeros((NB, w.shape[1] - NB), F32)
    first = split(inv)
    below = split(nt3(split(w[NB:, :NB]), first))
    w[NB:, NB:] = w[NB:, NB:] - nt3(below, below)
    mixed = split(nn3(below, first))
    inv = base_inverse(w[NB:, NB:], fill)
    h[NB:, NB:] = inv
    h[NB:, :NB] = -nn3(split(inv), mixed)


def factor_kernel(
    rows_n, cols_n, tile_cols, pts, prhs, opiv, ocolp, oh, orpiv, ok2, ol3, osq,
    piv, colp, rpiv, w, h0, h1, hs, own_pts, k2, l3, sq, send, recv, local, wsem,
):
    row_id = lax.axis_index("row")
    col_id = lax.axis_index("col")
    stride = cols_n // rows_n

    barrier = pltpu.get_barrier_semaphore()
    for step in range(1, rows_n):
        other = lax.rem(row_id + step, rows_n)
        pl.semaphore_signal(barrier, inc=1, device_id={"row": other}, device_id_type=MESH)

    jobs = [(0, pts.at[0, pl.ds(n * NB, NB)], piv.at[0, pl.ds(n * NB, NB)]) for n in range(2)]
    jobs += [(k % rows_n, pts.at[k // rows_n], piv.at[k]) for k in range(1, PANELS)]
    jobs += [(k % rows_n, prhs.at[k // rows_n], rpiv.at[k]) for k in range(PANELS)]
    for c2 in range(tile_cols):
        slot = c2 * stride + col_id // rows_n
        jobs.append((lax.rem(col_id, rows_n), pts.at[slot], colp.at[c2]))

    chips = rows_n // 2
    chip, core = row_id // 2, lax.rem(row_id, 2)
    sibling = row_id + 1 - 2 * core

    def half_of(ref, half):
        height = ref.shape[0] // 2
        return ref.at[pl.ds(pl.multiple_of(half * height, height), height)]

    def remote(number, half, dest, slot, relay=False):
        _, src, dst = jobs[number]
        if number in DIRECT:
            return pltpu.make_async_remote_copy(
                src_ref=src,
                dst_ref=dst,
                send_sem=send.at[number, slot],
                recv_sem=recv.at[number, 0],
                device_id={"row": dest},
                device_id_type=MESH,
            )
        return pltpu.make_async_remote_copy(
            src_ref=half_of(dst if relay else src, half),
            dst_ref=half_of(dst, half),
            send_sem=send.at[number, slot],
            recv_sem=recv.at[number, half],
            device_id={"row": dest},
            device_id_type=MESH,
        )

    def sends(number):
        out = []
        for step in range(1, chips):
            for half in (1, 0):
                dest = 2 * lax.rem(chip + step, chips) + half
                out.append(remote(number, half, dest, 2 * step + half))
        return out + [remote(number, half, sibling, half) for half in range(1 if number in DIRECT else 2)]

    def own(number):
        _, src, dst = jobs[number]
        return pltpu.make_async_copy(src, dst, local.at[number])

    def when(condition):
        return pl.when(condition)

    def launch(number):
        @when(row_id == jobs[number][0])
        def _():
            for copy in sends(number):
                copy.start()

    def relay(number):
        @when(chip != jobs[number][0] // 2)
        def _():
            copy = remote(number, core, sibling, 0, relay=True)
            copy.wait_recv()
            copy.start()

    def arrive(number):
        owner = jobs[number][0]

        @when(row_id == owner)
        def _():
            own(number).wait()

        if number in DIRECT:
            @when(row_id != owner)
            def _():
                remote(number, 0, sibling, 0).wait_recv()
            return

        @when(sibling == owner)
        def _():
            for half in range(2):
                remote(number, half, sibling, half).wait_recv()

        @when(chip != owner // 2)
        def _():
            remote(number, 1 - core, sibling, 0, relay=True).wait_recv()

    def drain(number):
        owner = jobs[number][0]

        @when(row_id == owner)
        def _():
            for copy in sends(number):
                copy.wait_send()

        if number in DIRECT:
            return

        @when(chip != owner // 2)
        def _():
            remote(number, core, sibling, 0, relay=True).wait_send()

    for number in range(len(jobs)):
        @when(row_id == jobs[number][0])
        def _(number=number):
            own(number).start()

    rows_copy = pltpu.make_async_copy(pts, own_pts, wsem.at[5])
    rows_copy.start()
    pl.semaphore_wait(barrier, rows_n - 1)
    launch(0)
    rows_copy.wait()
    side = along(own_pts[...].reshape(l3.shape[0], own_pts.shape[2]))
    l3[...] = side[0]
    sq[...] = jnp.broadcast_to(side[1], sq.shape)
    early = [pltpu.make_async_copy(l3, ol3, wsem.at[6]), pltpu.make_async_copy(sq, osq, wsem.at[7])]
    for copy in early:
        copy.start()
    relay(0)
    arrive(0)
    drain(0)
    launch(1)

    size = piv.shape[1]
    eye = (
        lax.broadcasted_iota(jnp.int32, (size, size), 0) == lax.broadcasted_iota(jnp.int32, (size, size), 1)
    ).astype(F32)

    def row_tiles(k):
        b = across(piv[k])
        step = own_pts.shape[0] * size * 16 // NB

        def piece(n):
            span = pl.ds(n * step, step)
            value = covariance((l3[span, :], widen(sq[span, :], size)), b)
            if n * step < size:
                value = value + jnp.where(row_id == k, NUGGET, 0.0) * eye[n * step : (n + 1) * step]
            hi, lo = split(value)
            k2[span, pl.ds(k * size, size)] = hi
            k2[span, pl.ds((PANELS + k) * size, size)] = lo

        return piece

    xa = piv[0, :NB]
    sqa = row_squares(xa)
    w[:NB, :NB] = squared_exp(xa, xa, sqa) + NUGGET * eye[:NB, :NB]
    inv = base_inverse(w[:NB, :NB])
    launch(2)
    for number in range(3, len(jobs)):
        launch(number)
    arrive(1)
    xb = piv[0, NB:]
    w[NB:, :NB] = squared_exp(xb, xa, sqa)
    w[NB:, NB:] = squared_exp(xb, xb, row_squares(xb)) + NUGGET * eye[:NB, :NB]
    x0 = piv[0]
    sq0 = row_squares(x0)
    inverse_factor(w, h0, inv, row_tiles(0))
    h0s = split(h0[...])
    hs[0, 0], hs[0, 1] = h0s
    arrive(2)
    x1 = piv[1]
    sq1 = row_squares(x1)
    l10s = split(nt3(split(squared_exp(x1, x0, sq0)), h0s))
    w[...] = squared_exp(x1, x1, sq1) + NUGGET * eye - nt3(l10s, l10s)
    mixed = split(nn3(l10s, h0s))
    inv = base_inverse(w[:NB, :NB], row_tiles(1))
    writes = [pltpu.make_async_copy(k2, ok2, wsem.at[4])]
    writes[0].start()
    for number in range(3, len(jobs)):
        relay(number)
    inverse_factor(w, h1, inv)
    for number in range(3, len(jobs)):
        arrive(number)
    writes += early + [
        pltpu.make_async_copy(src, dst, wsem.at[n]) for n, (src, dst) in enumerate(((piv, opiv), (colp, ocolp), (rpiv, orpiv)))
    ]
    for copy in writes[3:]:
        copy.start()
    h1s = split(h1[...])
    hs[1, 0], hs[1, 1] = h1s
    hs[2, 0], hs[2, 1] = split(-nn3(h1s, mixed))
    writes.append(pltpu.make_async_copy(hs, oh, wsem.at[3]))
    writes[-1].start()
    for number in range(1, len(jobs)):
        drain(number)
    for copy in writes:
        copy.wait()


def nn(a, b):
    return lax.dot_general(a, b, (((1,), (0,)), ((), ())), preferred_element_type=F32)


def nn3(a, b):
    return nn(a[0], b[0]) + (nn(a[0], b[1]) + nn(a[1], b[0]))


def scale_of(feat):
    return -SCALE / feat * LOG2E


def across(x):
    scale = scale_of(x.shape[1])
    return right3(x * (-2.0 * scale)), row_squares(x) * scale


def along(x):
    return left3(x), jnp.sum(x * x, axis=1, keepdims=True) * scale_of(x.shape[1])


def covariance(a, b):
    return jnp.exp2((nt(a[0], b[0]) + a[1]) + b[1])


def widen(x, size):
    return jnp.concatenate([x] * (size // x.shape[1]), axis=1)


def left3(x):
    hi, lo = split(x)
    return jnp.concatenate([hi, hi, lo], axis=1)


def right3(x):
    hi, lo = split(x)
    return jnp.concatenate([hi, lo, hi], axis=1)


def tiles_kernel(
    rows_n, cols_n, hpts, hpiv, hcolp, hrhs, hh, hr, hk2, hsq, out, solved,
    pts, sq, piv, colp, rhs, hs, rpiv, k2, lc3, stage, rest, sems, osems,
):
    row_id = lax.axis_index("row")
    col_id = lax.axis_index("col")
    copies = [
        pltpu.make_async_copy(src, dst, sems.at[n])
        for n, (src, dst) in enumerate(
            ((hpiv, piv), (hcolp, colp), (hpts, pts), (hh, hs), (hr, rpiv), (hk2, k2), (hrhs, rhs), (hsq, sq))
        )
    ]
    for copy in copies:
        copy.start()
    tile_cols, size, feat = colp.shape
    tile_rows = pts.shape[0] // size
    high, wide = tile_rows * size, tile_cols * size
    diagonal = lax.broadcasted_iota(jnp.int32, (size, size), 0) - lax.broadcasted_iota(
        jnp.int32, (size, size), 1
    )
    eye = (diagonal == 0).astype(F32)
    lower = diagonal >= 0

    def nugget(hit):
        return jnp.where(hit, NUGGET, 0.0) * eye

    for copy in copies[:2]:
        copy.wait()
    pivots = [across(piv[k]) for k in range(PANELS)]
    xc = colp[...].reshape(wide, feat)

    def spread(ref, value, k, order):
        pieces = split(value)
        for n, which in enumerate(order):
            ref[:, pl.ds((PANELS * n + k) * size, size)] = pieces[which]

    def pivot_tiles(x, tile):
        side = along(x)
        values = []
        for k in range(PANELS):
            value = covariance(side, pivots[k])
            values.append(jnp.concatenate([value[:size] + nugget(tile == k), value[size:]], axis=0))
        return values

    kc = pivot_tiles(xc, col_id)
    copies[3].wait()
    copies[4].wait()
    width = rpiv.shape[1]
    padding = [jnp.zeros((-width % 16, size), F32)] if width % 16 else []
    kc = [split(jnp.concatenate([kc[k], rpiv[k]] + padding, axis=0)) for k in range(PANELS)]
    h0s, h1s, hxs = ((hs[n, 0], hs[n, 1]) for n in range(3))
    l0 = nt3(kc[0], h0s)
    l1 = nt3(kc[0], hxs) + nt3(kc[1], h1s)
    l0s, l1s = split(l0), split(l1)
    weighted = nn3(l0s, h0s) + nn3(l1s, hxs), nn3(l1s, h1s)
    for k in range(PANELS):
        spread(lc3, weighted[k][:wide], k, (0, 1, 0))
    ys = l0[wide : wide + width], l1[wide : wide + width]
    z = split(jnp.concatenate([value[wide : wide + width] for value in weighted], axis=1))
    copies[2].wait()
    copies[7].wait()
    copies[5].wait()

    def stacked(begin, end):
        span = pl.ds(begin * size, (end - begin) * size)
        return jnp.concatenate([k2[span, : PANELS * size], k2[span, :]], axis=1)

    def put(a, c2, value):
        for half in range(size // 128):
            stage[a, pl.ds(c2 * (size // 128) + half, size, stride=wide // 128), :] = value[
                :, half * 128 : half * 128 + 128
            ]

    def schur(c2, begin, end):
        tile_c = c2 * cols_n + col_id
        value = covariance((pts[begin * size : end * size, :], widen(sq[begin * size : end * size, :], size)), across(colp[c2]))
        value = value - nt(stacked(begin, end), lc3[c2 * size : (c2 + 1) * size, :])
        for a in range(begin, end):
            tile = a * rows_n + row_id
            part = value[(a - begin) * size : (a - begin + 1) * size] + nugget(tile == tile_c)
            put(a, c2, jnp.where(tile >= PANELS, part, 0.0) if a == 0 else part)

    @pl.when(col_id >= PANELS)
    def _():
        schur(0, 0, tile_rows)

    def panel(k):
        halves = [
            (k2[:, j * size : (j + 1) * size], k2[:, (PANELS + j) * size : (PANELS + j + 1) * size])
            for j in range(PANELS)
        ]
        value = nt3(halves[0], h0s) if k == 0 else nt3(halves[0], hxs) + nt3(halves[1], h1s)
        top = jnp.where((row_id > k) | (lower & (row_id == k)), value[:size], 0.0)
        for a in range(tile_rows):
            put(a, 0, value[a * size : (a + 1) * size] if a else top)

    for k in range(PANELS):

        @pl.when(col_id == k)
        def _(k=k):
            panel(k)

    copies[6].wait()
    z = [piece.astype(F32) for piece in z]
    room = max(NB, 2 * width)
    filled = jnp.concatenate(
        [jnp.concatenate([piece, piece], axis=1) for piece in z]
        + ([jnp.zeros((room - 2 * width, 2 * PANELS * size), F32)] if room > 2 * width else []),
        axis=0,
    ).astype(BF16)
    update = nt(k2[...], filled)
    for a in range(tile_rows):
        tile = a * rows_n + row_id
        turned = jnp.concatenate(
            [update[a * size + n : a * size + n + 128].T for n in range(0, size, 128)], axis=1
        )
        value = rhs[a] - (turned[:width] + turned[width : 2 * width])
        if a == 0:
            for k in range(PANELS):
                value = jnp.where(tile == k, ys[k], value)
        rest[a] = value
    writes = [pltpu.make_async_copy(rest, solved, osems.at[tile_rows])]
    writes[0].start()

    for c2 in range(1, tile_cols):
        for begin in range(0, tile_rows, 2):
            end = min(begin + 2, tile_rows)
            schur(c2, begin, end)
            if c2 == tile_cols - 1:
                for a in range(begin, end):
                    writes.append(pltpu.make_async_copy(stage.at[a], out.at[a], osems.at[a]))
                    writes[-1].start()
    for copy in writes:
        copy.wait()


def per_device(points, rhs):
    rows_n = lax.axis_size("row")
    cols_n = lax.axis_size("col")
    tile_rows, _, size, feat = points.shape
    width = rhs.shape[-1]
    tile_cols = tile_rows * rows_n // cols_n
    pts = points[:, 0]
    right = rhs[:, 0].swapaxes(1, 2)
    jobs = 2 * PANELS + tile_cols + 1
    hbm = pl.BlockSpec(memory_space=pltpu.HBM)
    piv_s, colp_s = (PANELS, size, feat), (tile_cols, size, feat)
    h_s, r_s = (3, 2, size, size), (PANELS, width, size)
    k_s = (tile_rows * size, 2 * PANELS * size)
    l_s, q_s = (tile_rows * size, 3 * feat), (tile_rows * size, 128)
    piv, colp, hs, rpiv, k2, l3, sq = pl.pallas_call(
        functools.partial(factor_kernel, rows_n, cols_n, tile_cols),
        out_shape=(
            jax.ShapeDtypeStruct(piv_s, F32),
            jax.ShapeDtypeStruct(colp_s, F32),
            jax.ShapeDtypeStruct(h_s, BF16),
            jax.ShapeDtypeStruct(r_s, F32),
            jax.ShapeDtypeStruct(k_s, BF16),
            jax.ShapeDtypeStruct(l_s, BF16),
            jax.ShapeDtypeStruct(q_s, F32),
        ),
        in_specs=[hbm] * 2,
        out_specs=(hbm,) * 7,
        scratch_shapes=[
            pltpu.VMEM(piv_s, F32),
            pltpu.VMEM(colp_s, F32),
            pltpu.VMEM(r_s, F32),
            pltpu.VMEM((size, size), F32),
            pltpu.VMEM((size, size), F32),
            pltpu.VMEM((size, size), F32),
            pltpu.VMEM(h_s, BF16),
            pltpu.VMEM(pts.shape, F32),
            pltpu.VMEM(k_s, BF16),
            pltpu.VMEM(l_s, BF16),
            pltpu.VMEM(q_s, F32),
            pltpu.SemaphoreType.DMA((jobs, rows_n)),
            pltpu.SemaphoreType.DMA((jobs, 2)),
            pltpu.SemaphoreType.DMA((jobs,)),
            pltpu.SemaphoreType.DMA((8,)),
        ],
        compiler_params=pltpu.CompilerParams(
            collective_id=0, has_side_effects=True, vmem_limit_bytes=62 * 1024 * 1024
        ),
        name="factor",
    )(pts, right)
    out_s = (tile_rows, size * tile_cols * size // 128, 128)
    factored, solved = pl.pallas_call(
        functools.partial(tiles_kernel, rows_n, cols_n),
        out_shape=(
            jax.ShapeDtypeStruct(out_s, F32),
            jax.ShapeDtypeStruct((tile_rows, width, size), F32),
        ),
        in_specs=[hbm] * 8,
        out_specs=(hbm,) * 2,
        scratch_shapes=[
            pltpu.VMEM(l_s, BF16),
            pltpu.VMEM(q_s, F32),
            pltpu.VMEM(piv_s, F32),
            pltpu.VMEM(colp_s, F32),
            pltpu.VMEM(right.shape, F32),
            pltpu.VMEM(h_s, BF16),
            pltpu.VMEM(r_s, F32),
            pltpu.VMEM(k_s, BF16),
            pltpu.VMEM((tile_cols * size, 3 * PANELS * size), BF16),
            pltpu.VMEM(out_s, F32),
            pltpu.VMEM((tile_rows, width, size), F32),
            pltpu.SemaphoreType.DMA((8,)),
            pltpu.SemaphoreType.DMA((tile_rows + 1,)),
        ],
        compiler_params=pltpu.CompilerParams(vmem_limit_bytes=62 * 1024 * 1024),
        name="tiles",
    )(l3, piv, colp, right, hs, rpiv, k2, sq)
    factored = factored.reshape(tile_rows, 1, size, tile_cols, 1, size)
    return factored, solved.swapaxes(1, 2)[:, None]


def solution(mesh):
    return jax.shard_map(
        per_device,
        mesh=mesh,
        in_specs=(P(None, "row", None, None), P(None, "row", None, "col")),
        out_specs=(P(None, "row", None, None, "col", None), P(None, "row", None, "col")),
        check_vma=False,
    )
```
